512 devices in a mesh: scene: 4 (over x), dom: 128 (over y, z, core).
Axes of the slice: x: 4, y: 4, z: 16, core: 2. Of those that a mesh axis runs over, the one named last changes fastest.
Arguments:
- features: bfloat16 [1024, 8, 8, 512], P(('scene', 'dom')), parts along dimension 0, may hold values from -5 to 5
- weight_first: bfloat16 [3, 3, 3, 64, 64], replicated, may hold values from -0.15625 to 0.15625
- weight_second: bfloat16 [3, 3, 3, 64, 64], replicated, may hold values from -0.15625 to 0.15625
- neighbours: int32 [1024, 26], P(('scene', 'dom')), parts along dimension 0, may hold values from -1 to 255, as said below
- active: int32 [1024], P(('scene', 'dom')), parts along dimension 0, may hold values from 0 to 1, as said below
- cotangent: bfloat16 [1024, 8, 8, 512], P(('scene', 'dom')), parts along dimension 0, may hold values from -5 to 5
Outputs:
- output: bfloat16 [1024, 8, 8, 512], P(('scene', 'dom')), parts along dimension 0
- grad_features: bfloat16 [1024, 8, 8, 512], P(('scene', 'dom')), parts along dimension 0
- filter_grad_first: float32 [12, 3, 3, 64, 64], P('scene'), parts along dimension 0
- filter_grad_second: float32 [12, 3, 3, 64, 64], P('scene'), parts along dimension 0
The draws below stay inside these ranges and needn't reach their ends.
There are 4 independent parts, one for each index of `scene`. The reference program is written for one: setup_inputs(seed, part) draws one part's arguments, and reference() takes and returns one part's arrays. A program takes and returns all parts, laid end to end along the dimension named above; an argument that names none is the same for every part. Nothing has to cross between parts.
Inputs may be any that keep to these rules, and one draw needn't show every extreme that they name: `neighbours`: offsets (dx, dy, dz) run over the finite set (-1, 0, 1) cubed without (0, 0, 0), in lexicographic order with dx slowest. Entry k of row b is the id of the active brick whose voxels continue those of brick b at offset k, or -1; rows of inactive bricks are all -1. The relation is symmetric: b lists c at an offset exactly when c lists b at the opposite one. A brick listed at dx = 0 has the same id // 2 as b; at dx = -1 or +1 its id // 2 is one lower or one higher. Some index of dom has all of its 2 slots active.
All inputs are finite; a program needn't handle non-finite values.
Results may differ from the reference program's by a relative error of at most 0.0035.
Values may be sent and summed in bfloat16 or wider, within the bound.
A program may use at most 64 MiB of HBM per device.

```python
import math
import jax
import jax.numpy as jnp
from jax import lax

C = 64
E = 8
SY = 2
SZ = 1
SLOTS = 2
NB = 256


def brick_layout(key):
    key_order, key_rate, key_roll, key_full = jax.random.split(key, 4)
    device_count = NB // SLOTS
    orders = jax.vmap(lambda subkey: jax.random.permutation(subkey, SLOTS))(jax.random.split(key_order, device_count)).astype(jnp.int32)
    places = jnp.argsort(orders, axis=1, stable=True).astype(jnp.int32)
    rates = jax.random.randint(key_rate, (device_count, 1), 1, 5)
    rolls = jax.random.randint(key_roll, (device_count, SLOTS), 0, 4)
    filled = jax.random.randint(key_full, (), 0, device_count)
    devices = jnp.arange(device_count, dtype=jnp.int32)[:, None]
    alive_pos = (rolls < rates) | (devices == filled)
    alive = jnp.take_along_axis(alive_pos, orders, axis=1)
    coord_y = orders // SZ
    coord_z = orders % SZ
    columns = []
    for step_x in (-1, 0, 1):
        for step_y in (-1, 0, 1):
            for step_z in (-1, 0, 1):
                if (step_x, step_y, step_z) == (0, 0, 0):
                    continue
                near_dev = devices + step_x
                near_y = coord_y + step_y
                near_z = coord_z + step_z
                inside = (near_dev >= 0) & (near_dev < device_count) & (near_y >= 0) & (near_y < SY) & (near_z >= 0) & (near_z < SZ)
                dev_clip = jnp.clip(near_dev, 0, device_count - 1)
                pos_clip = jnp.clip(near_y, 0, SY - 1) * SZ + jnp.clip(near_z, 0, SZ - 1)
                dev_full = jnp.broadcast_to(dev_clip, pos_clip.shape)
                there = alive_pos[dev_full, pos_clip]
                slot_near = places[dev_full, pos_clip]
                usable = inside & there & alive
                columns.append(jnp.where(usable, dev_full * SLOTS + slot_near, -1))
    neighbours = jnp.stack(columns, axis=-1).reshape(NB, 26).astype(jnp.int32)
    return (alive.reshape(NB).astype(jnp.int32), neighbours)


def field_values(key):
    values = jnp.clip(jax.random.normal(key, (NB, E, E, E * C), jnp.float32), -5.0, 5.0)
    return values.astype(jnp.bfloat16)


def draw_neighbours(key, part):
    return brick_layout(key)[1]


def draw_active(key, part):
    return brick_layout(key)[0]


def draw_features(key, part):
    key = jax.random.fold_in(key, 7)
    return field_values(key)


def draw_cotangent(key, part):
    key = jax.random.fold_in(key, 13)
    return field_values(key)


def normal_values(own_key, extent, spread, limit, held_as=jnp.bfloat16):
    values = spread * jax.random.normal(own_key, extent, jnp.float32)
    return jnp.clip(values, min=-limit, max=limit).astype(held_as)


def setup_inputs(seed: int = 0, part: int = 0) -> dict:
    key_list = jax.random.split(jax.random.key(seed), 7)
    own_keys = jax.random.split(jax.random.fold_in(key_list[6], part), 7)
    return {
        "features": draw_features(jax.random.fold_in(jax.random.fold_in(key_list[6], part), 71), part),
        "weight_first": normal_values(key_list[1], (3, 3, 3, C, C), (27 * C) ** -0.5, 0.15625),
        "weight_second": normal_values(key_list[2], (3, 3, 3, C, C), (27 * C) ** -0.5, 0.15625),
        "neighbours": draw_neighbours(jax.random.fold_in(jax.random.fold_in(key_list[6], part), 71), part),
        "active": draw_active(jax.random.fold_in(jax.random.fold_in(key_list[6], part), 71), part),
        "cotangent": draw_cotangent(jax.random.fold_in(jax.random.fold_in(key_list[6], part), 71), part),
    }


def directions():
    offsets_all = []
    for step_x in (-1, 0, 1):
        for step_y in (-1, 0, 1):
            for step_z in (-1, 0, 1):
                if (step_x, step_y, step_z) != (0, 0, 0):
                    offsets_all.append((step_x, step_y, step_z))
    return offsets_all

def source_range(offset, length):
    if offset < 0:
        return (length - 1, length)
    if offset > 0:
        return (0, 1)
    return (0, length)

def join_blocks(blocks):
    planes = []
    for step_x in (-1, 0, 1):
        row_list = []
        for step_y in (-1, 0, 1):
            row_list.append(jnp.concatenate([blocks[step_x, step_y, step_z] for step_z in (-1, 0, 1)], axis=3))
        planes.append(jnp.concatenate(row_list, axis=2))
    return jnp.concatenate(planes, axis=1)

def pad_bricks(bricks, neighbours):
    brick_count = bricks.shape[0]
    extended = jnp.concatenate([bricks, jnp.zeros((1,) + bricks.shape[1:], bricks.dtype)], axis=0)
    lookup = jnp.where(neighbours < 0, brick_count, neighbours).astype(jnp.int32)
    blocks = {(0, 0, 0): bricks}
    for number, offset in enumerate(directions()):
        range_x = source_range(offset[0], E)
        range_y = source_range(offset[1], E)
        range_z = source_range(offset[2], E)
        portion = extended[:, range_x[0]:range_x[1], range_y[0]:range_y[1], range_z[0]:range_z[1]]
        blocks[offset] = jnp.take(portion, lookup[:, number], axis=0)
    return join_blocks(blocks)

def convolve(padded, kernel):
    return lax.conv_general_dilated(padded, kernel, (1, 1, 1), 'VALID', dimension_numbers=('NDHWC', 'DHWIO', 'NDHWC'), preferred_element_type=jnp.float32)

def flip_kernel(kernel):
    return jnp.flip(kernel, (0, 1, 2)).transpose(0, 1, 2, 4, 3)

def weight_grad(padded, grads):
    tap_list = []
    wide = grads.astype(jnp.float32)
    for shift_x in range(3):
        for shift_y in range(3):
            for shift_z in range(3):
                window = padded[:, shift_x:shift_x + E, shift_y:shift_y + E, shift_z:shift_z + E].astype(jnp.float32)
                tap_list.append(jnp.einsum('nxyzi,nxyzo->io', window, wide, precision=lax.Precision.HIGHEST))
    return jnp.stack(tap_list).reshape(3, 3, 3, C, C)

def silu_slope(inputs):
    sigmoid_val = jax.nn.sigmoid(inputs)
    return sigmoid_val * (1.0 + inputs * (1.0 - sigmoid_val))

def reference(features, weight_first, weight_second, neighbours, active, cotangent):
    brick_count = features.shape[0]
    bricks = features.reshape(brick_count, E, E, E, C)
    grad_given = cotangent.reshape(brick_count, E, E, E, C)
    alive_mask = active.astype(jnp.float32).reshape(brick_count, 1, 1, 1, 1)
    padded_in = pad_bricks(bricks, neighbours)
    hidden_pre = convolve(padded_in, weight_first)
    middle = (alive_mask * jax.nn.silu(hidden_pre)).astype(jnp.bfloat16)
    padded_mid = pad_bricks(middle, neighbours)
    block_out = convolve(padded_mid, weight_second)
    output = (bricks.astype(jnp.float32) + block_out).astype(jnp.bfloat16)
    grad_out = (alive_mask * grad_given.astype(jnp.float32)).astype(jnp.bfloat16)
    grad_middle = convolve(pad_bricks(grad_out, neighbours), flip_kernel(weight_second))
    grad_hidden = (grad_middle * silu_slope(hidden_pre)).astype(jnp.bfloat16)
    grad_input = convolve(pad_bricks(grad_hidden, neighbours), flip_kernel(weight_first))
    grad_features = (alive_mask * (grad_given.astype(jnp.float32) + grad_input)).astype(jnp.bfloat16)
    grad_scale = 1.0 / math.sqrt(NB * E ** 3)
    filter_grad_first = weight_grad(padded_in, grad_hidden) * grad_scale
    filter_grad_second = weight_grad(padded_mid, grad_out) * grad_scale
    return (output.reshape(features.shape), grad_features.reshape(features.shape), filter_grad_first, filter_grad_second)
```

```python
import functools
import math

import jax
import jax.numpy as jnp
from jax import lax
from jax.experimental import pallas as pl
from jax.experimental.pallas import tpu as pltpu
from jax.sharding import PartitionSpec as P

C = 64
E = 8
FEAT, GOUT, MID, GHID = 0, 1, 2, 3
TN = (((0,), (0,)), ((), ()))
NT = (((1,), (1,)), ((), ()))
ROWS = 27 * C
HALF = ROWS // 2
CH = 16
NCORE = 2
NZ = 16


def entry(nb, brick, offset):
    if offset == (0, 0, 0):
        return 8 * brick
    place = (offset[0] + 1) * 9 + (offset[1] + 1) * 3 + offset[2] + 1
    ident = nb[brick, place if place < 13 else place - 1]
    return jnp.where(ident < 0, -1000, (ident & 1) * 8)


def build_selection(nb, sel):
    row = lax.broadcasted_iota(jnp.int32, (16, 160), 0)
    lane = lax.broadcasted_iota(jnp.int32, (16, 160), 1)
    y = row & 7
    second = row >= 8
    for iz in range(3):
        for c in range(3):
            yy = y + (c - 1)
            wrap = (yy < 0) | (yy > 7)
            for ix in range(3):
                codes = []
                for brick in range(2):
                    inner = entry(nb, brick, (ix - 1, 0, iz - 1))
                    if c == 1:
                        codes.append(jnp.full((16, 160), inner, jnp.int32))
                    else:
                        outer = entry(nb, brick, (ix - 1, c - 1, iz - 1))
                        codes.append(jnp.where(wrap, outer, inner))
                target = jnp.where(second, codes[1], codes[0]) + (yy & 7)
                for x in ((0,), tuple(range(1, 9)), (9,))[ix]:
                    hit = lane == target + 16 * x
                    sel[iz, 160 * c + 16 * x : 160 * c + 16 * x + 16, :] = jnp.where(
                        hit, 1.0, 0.0
                    ).astype(jnp.bfloat16)


def build_bands(weight, band, band_t):
    zero = jnp.zeros((C, C), jnp.bfloat16)
    for t in range(9):
        taps = [weight[3 * t + e] for e in range(3)]
        for zi in range(4):
            left = taps[zi] if zi < 3 else zero
            right = taps[zi - 1] if zi > 0 else zero
            band[t, C * zi : C * zi + C, :] = jnp.concatenate([left, right], axis=1)
        band_t[8 - t, :C, :] = jnp.concatenate([taps[2], taps[1], taps[0], zero], axis=1)
        band_t[8 - t, C:, :] = jnp.concatenate([zero, taps[2], taps[1], taps[0]], axis=1)


def build_padded(field, raw, sel, padded):
    source = raw[field].reshape(160, 512).astype(jnp.float32)
    source = pltpu.roll(source, C, 1).astype(jnp.bfloat16)
    edge = source[:, :128]
    low = lax.broadcasted_iota(jnp.int32, (480, 128), 1) < C
    inner = jnp.dot(sel[1], source, preferred_element_type=jnp.float32)
    before = jnp.dot(sel[0], edge, preferred_element_type=jnp.float32)
    after = jnp.dot(sel[2], edge, preferred_element_type=jnp.float32)
    padded[field, :, 128:512] = inner[:, 128:].astype(jnp.bfloat16)
    padded[field, :, :128] = jnp.where(low, before, inner[:, :128]).astype(jnp.bfloat16)
    padded[field, :, 512:] = jnp.where(low, inner[:, :128], after).astype(jnp.bfloat16)


def window(padded, field, t, pair):
    a, c = t // 3, t % 3
    start = 160 * c + 16 * a
    return padded[field, start : start + 128, 128 * pair : 128 * pair + 256]


def convolve(padded, field, band, pair, flipped):
    total = None
    for t in range(9):
        part = window(padded, field, t, pair)
        if flipped:
            term = lax.dot_general(part, band[t], NT, preferred_element_type=jnp.float32)
        else:
            term = jnp.dot(part, band[t], preferred_element_type=jnp.float32)
        total = term if total is None else total + term
    return total


def kernel(
    ny, nz, scale,
    feat, wa, wb, nb, act, cot,
    out, gfeat, fa, fb,
    raw, sel, padded, band_a, band_at, band_b, band_bt, sums, from_core, from_y, ysum, from_z, full,
    halo_send, halo_recv, core_send, core_recv, y_send, y_recv, z_send, z_recv,
    gz_send, gz_recv, gy_send, gy_recv, gc_send, gc_recv,
):
    count = ny * nz * NCORE
    me = lax.axis_index("dom")
    core = me % NCORE
    z = (me // NCORE) % nz
    y = me // (NCORE * nz)
    up = (me + 1) % count
    down = (me + count - 1) % count
    partner = me + 1 - 2 * core

    def at_y(step):
        return (((y + step) % ny) * nz + z) * NCORE + core

    def at_z(step):
        return (y * nz + (z + step) % nz) * NCORE + core

    barrier = pltpu.get_barrier_semaphore()
    pl.semaphore_signal(barrier, inc=1, device_id={"dom": up})
    pl.semaphore_signal(barrier, inc=1, device_id={"dom": down})
    for step in range(1, ny):
        pl.semaphore_signal(barrier, inc=1, device_id={"dom": at_y(step)})

    def greet(step, carry):
        pl.semaphore_signal(barrier, inc=1, device_id={"dom": at_z(step)})
        return carry

    lax.fori_loop(1, nz, greet, 0)

    keep = [jnp.where(act[b] > 0, 1.0, 0.0) for b in range(2)]
    rows = lax.broadcasted_iota(jnp.int32, (128, 128), 0)
    alive = jnp.where((rows & 8) == 0, keep[0], keep[1])
    raw[FEAT, 1:9] = jnp.concatenate(
        [feat[b].astype(jnp.float32) for b in range(2)], axis=1
    ).astype(jnp.bfloat16)
    raw[GOUT, 1:9] = jnp.concatenate(
        [cot[b].astype(jnp.float32) * keep[b] for b in range(2)], axis=1
    ).astype(jnp.bfloat16)

    def halo(number):
        copies = []
        for way, (source, target, device) in enumerate(((8, 0, up), (1, 9, down))):
            copies.append(
                pltpu.make_async_remote_copy(
                    src_ref=raw.at[2 * number : 2 * number + 2, source],
                    dst_ref=raw.at[2 * number : 2 * number + 2, target],
                    send_sem=halo_send.at[2 * number + way],
                    recv_sem=halo_recv.at[2 * number + way],
                    device_id={"dom": device},
                )
            )
        return copies

    pl.semaphore_wait(barrier, 2 + (ny - 1) + (nz - 1))
    first = halo(0)
    for copy in first:
        copy.start()
    build_selection(nb, sel)
    build_bands(wa, band_a, band_at)
    build_bands(wb, band_b, band_bt)
    for copy in first:
        copy.wait()

    build_padded(FEAT, raw, sel, padded)
    build_padded(GOUT, raw, sel, padded)
    for pair in range(4):
        lanes = slice(128 * pair, 128 * pair + 128)
        hidden = convolve(padded, FEAT, band_a, pair, False)
        grad = convolve(padded, GOUT, band_bt, pair, True)
        s = jax.nn.sigmoid(hidden)
        middle = alive * (hidden * s)
        ghid = grad * (s * (1.0 + hidden * (1.0 - s)))
        raw[MID, 1:9, :, lanes] = middle.astype(jnp.bfloat16).reshape(8, 16, 128)
        raw[GHID, 1:9, :, lanes] = ghid.astype(jnp.bfloat16).reshape(8, 16, 128)
    second = halo(1)
    for copy in second:
        copy.start()

    low = lax.broadcasted_iota(jnp.int32, (C, 128), 1) < C
    for t in range(9):
        one = None
        two = None
        for pair in range(4):
            lanes = slice(128 * pair, 128 * pair + 128)
            ghid = raw[GHID, 1:9, :, lanes].reshape(128, 128)
            middle = raw[MID, 1:9, :, lanes].reshape(128, 128)
            term = lax.dot_general(
                window(padded, FEAT, t, pair), ghid, TN, preferred_element_type=jnp.float32
            )
            one = term if one is None else one + term
            term = lax.dot_general(
                middle, window(padded, GOUT, 8 - t, pair), TN, preferred_element_type=jnp.float32
            )
            two = term if two is None else two + term
        straight = two[:C]
        moved = two[C:]
        for e in range(3):
            near = one[C * e : C * e + C]
            far = one[C * e + C : C * e + 2 * C]
            flip = 2 - e
            pieces = []
            for value, block in ((straight, flip), (moved, flip + 1)):
                tile = value[:, 128 * (block // 2) : 128 * (block // 2) + 128]
                pieces.append(tile if block % 2 else pltpu.roll(tile, C, 1))
            first_part = near + pltpu.roll(far, C, 1)
            second_part = pieces[0] + pieces[1]
            start = 192 * t + C * e
            sums[start : start + C, :] = jnp.where(low, first_part, second_part)

    own = pl.multiple_of(core * HALF, 8)
    other = pl.multiple_of((1 - core) * HALF, 8)
    to_core = pltpu.make_async_remote_copy(
        src_ref=sums.at[pl.ds(other, HALF)],
        dst_ref=from_core,
        send_sem=core_send,
        recv_sem=core_recv,
        device_id={"dom": partner},
    )
    to_core.start()
    for copy in second:
        copy.wait()
    build_padded(MID, raw, sel, padded)
    build_padded(GHID, raw, sel, padded)
    to_core.wait()
    ylen = HALF // ny
    from_core[...] = from_core[...] + sums[pl.ds(own, HALF), :]

    y_copies = []
    for step in range(1, ny):
        begin = pl.multiple_of(((y + step) % ny) * ylen, 8)
        y_copies.append(
            pltpu.make_async_remote_copy(
                src_ref=from_core.at[pl.ds(begin, ylen)],
                dst_ref=from_y.at[step - 1],
                send_sem=y_send.at[step - 1],
                recv_sem=y_recv.at[step - 1],
                device_id={"dom": at_y(step)},
            )
        )
    for copy in y_copies:
        copy.start()

    def last(field, band, flipped, target, base, masked):
        for pair in range(4):
            lanes = slice(128 * pair, 128 * pair + 128)
            value = convolve(padded, field, band, pair, flipped)
            if masked:
                value = value * alive
            value = value.reshape(8, 16, 128)
            for b in range(2):
                given = base[b, :, :, lanes].astype(jnp.float32)
                if masked:
                    given = given * keep[b]
                target[b, :, :, lanes] = (given + value[:, 8 * b : 8 * b + 8]).astype(jnp.bfloat16)

    last(MID, band_b, False, out, feat, False)
    for copy in y_copies:
        copy.wait()
    mine = pl.multiple_of(y * ylen, 8)
    total = from_core[pl.ds(mine, ylen), :]
    for step in range(1, ny):
        total = total + from_y[step - 1]
    ysum[:ylen, :] = total
    if ylen < CH * nz:
        ysum[ylen:, :] = jnp.zeros((CH * nz - ylen, 128), jnp.float32)

    def z_copy(step):
        begin = pl.multiple_of(((z + step) % nz) * CH, CH)
        return pltpu.make_async_remote_copy(
            src_ref=ysum.at[pl.ds(begin, CH)],
            dst_ref=from_z.at[step - 1],
            send_sem=z_send.at[step - 1],
            recv_sem=z_recv.at[step - 1],
            device_id={"dom": at_z(step)},
        )

    def g_copy(step):
        return pltpu.make_async_remote_copy(
            src_ref=full.at[core, y, z],
            dst_ref=full.at[core, y, z],
            send_sem=gz_send.at[step - 1],
            recv_sem=gz_recv.at[step - 1],
            device_id={"dom": at_z(step)},
        )

    def start_all(make):
        def body(step, carry):
            make(step).start()
            return carry

        lax.fori_loop(1, nz, body, 0)

    def wait_all(make):
        def body(step, carry):
            make(step).wait()
            return carry

        lax.fori_loop(1, nz, body, 0)

    start_all(z_copy)
    last(GHID, band_at, True, gfeat, cot, True)
    wait_all(z_copy)
    total = ysum[pl.ds(pl.multiple_of(z * CH, CH), CH), :]
    for step in range(1, nz):
        total = total + from_z[step - 1]
    full[core, y, z] = (total * scale).astype(jnp.bfloat16)
    start_all(g_copy)
    wait_all(g_copy)

    gy_copies = []
    for step in range(1, ny):
        gy_copies.append(
            pltpu.make_async_remote_copy(
                src_ref=full.at[core, y],
                dst_ref=full.at[core, y],
                send_sem=gy_send.at[step - 1],
                recv_sem=gy_recv.at[step - 1],
                device_id={"dom": at_y(step)},
            )
        )
    for copy in gy_copies:
        copy.start()
    for copy in gy_copies:
        copy.wait()
    gc_copy = pltpu.make_async_remote_copy(
        src_ref=full.at[core],
        dst_ref=full.at[core],
        send_sem=gc_send,
        recv_sem=gc_recv,
        device_id={"dom": partner},
    )
    gc_copy.start()
    gc_copy.wait()
    for h in range(NCORE):
        for j in range(ny):
            value = full[h, j].reshape(CH * nz, 128)[:ylen, :].astype(jnp.float32)
            begin = h * HALF + j * ylen
            fa[begin : begin + ylen, :] = value[:, :C]
            fb[begin : begin + ylen, :] = pltpu.roll(value, C, 1)[:, :C]


def on_device(ny, nz, features, weight_first, weight_second, neighbours, active, cotangent):
    count = ny * nz * NCORE
    scale = 1.0 / math.sqrt(2 * count * E**3)
    vmem = pl.BlockSpec(memory_space=pltpu.VMEM)
    smem = pl.BlockSpec(memory_space=pltpu.SMEM)
    bf16, f32 = jnp.bfloat16, jnp.float32
    dma = pltpu.SemaphoreType.DMA
    out, gfeat, fa, fb = pl.pallas_call(
        functools.partial(kernel, ny, nz, scale),
        out_shape=(
            jax.ShapeDtypeStruct(features.shape, bf16),
            jax.ShapeDtypeStruct(features.shape, bf16),
            jax.ShapeDtypeStruct((ROWS, C), f32),
            jax.ShapeDtypeStruct((ROWS, C), f32),
        ),
        in_specs=[vmem, vmem, vmem, smem, smem, vmem],
        out_specs=(vmem, vmem, vmem, vmem),
        scratch_shapes=[
            pltpu.VMEM((4, 10, 16, 512), bf16),
            pltpu.VMEM((3, 480, 160), bf16),
            pltpu.VMEM((4, 480, 640), bf16),
            pltpu.VMEM((9, 256, 128), bf16),
            pltpu.VMEM((9, 128, 256), bf16),
            pltpu.VMEM((9, 256, 128), bf16),
            pltpu.VMEM((9, 128, 256), bf16),
            pltpu.VMEM((ROWS, 128), f32),
            pltpu.VMEM((HALF, 128), f32),
            pltpu.VMEM((ny - 1, HALF // ny, 128), f32),
            pltpu.VMEM((CH * nz, 128), f32),
            pltpu.VMEM((nz - 1, CH, 128), f32),
            pltpu.VMEM((NCORE, ny, nz, CH, 128), bf16),
            dma((4,)), dma((4,)),
            dma, dma,
            dma((ny - 1,)), dma((ny - 1,)),
            dma((nz - 1,)), dma((nz - 1,)),
            dma((nz - 1,)), dma((nz - 1,)),
            dma((ny - 1,)), dma((ny - 1,)),
            dma, dma,
        ],
        compiler_params=pltpu.CompilerParams(
            collective_id=0, has_side_effects=True, vmem_limit_bytes=40 * 2**20
        ),
    )(
        features,
        weight_first.reshape(27, C, C),
        weight_second.reshape(27, C, C),
        neighbours,
        active,
        cotangent,
    )
    return out, gfeat, fa.reshape(3, 3, 3, C, C), fb.reshape(3, 3, 3, C, C)


def solution(mesh):
    count = mesh.shape["dom"]
    return jax.shard_map(
        functools.partial(on_device, count // (NZ * NCORE), NZ),
        mesh=mesh,
        in_specs=(
            P(("scene", "dom"), None, None, None),
            P(),
            P(),
            P(("scene", "dom"), None),
            P(("scene", "dom")),
            P(("scene", "dom"), None, None, None),
        ),
        out_specs=(
            P(("scene", "dom"), None, None, None),
            P(("scene", "dom"), None, None, None),
            P("scene", None, None, None, None),
            P("scene", None, None, None, None),
        ),
        check_vma=False,
    )
```

```python
import functools
import math

import jax
import jax.numpy as jnp
from jax import lax
from jax.experimental import pallas as pl
from jax.experimental.pallas import tpu as pltpu
from jax.sharding import PartitionSpec as P

C = 64
E = 8
FEAT, GOUT, MID, GHID = 0, 1, 2, 3
TN = (((0,), (0,)), ((), ()))
NT = (((1,), (1,)), ((), ()))
ROWS = 27 * C
HALF = ROWS // 2
NCORE = 2
NZ = 16
ZLOW = 4
CH = 64
F32 = jnp.float32
BF16 = jnp.bfloat16


def entry(nb, brick, offset):
    if offset == (0, 0, 0):
        return 8 * brick
    place = (offset[0] + 1) * 9 + (offset[1] + 1) * 3 + offset[2] + 1
    ident = nb[brick, place if place < 13 else place - 1]
    return jnp.where(ident < 0, -1000, (ident & 1) * 8)


def build_selection(nb, sel, sel_edge):
    row = lax.broadcasted_iota(jnp.int32, (16, 128), 0)
    lane = lax.broadcasted_iota(jnp.int32, (16, 128), 1)
    y = row & 7
    second = row >= 8
    for iz in range(3):
        for c in range(3):
            yy = y + (c - 1)
            wrap = (yy < 0) | (yy > 7)
            for ix in range(3):
                codes = []
                for brick in range(2):
                    inner = entry(nb, brick, (ix - 1, 0, iz - 1))
                    if c == 1:
                        codes.append(jnp.full((16, 128), inner, jnp.int32))
                    else:
                        outer = entry(nb, brick, (ix - 1, c - 1, iz - 1))
                        codes.append(jnp.where(wrap, outer, inner))
                target = jnp.where(second, codes[1], codes[0]) + (yy & 7)
                if ix == 1:
                    for x in range(8):
                        hit = jnp.where(lane == target + 16 * x, 1.0, 0.0).astype(BF16)
                        sel[iz, 128 * c + 16 * x : 128 * c + 16 * x + 16, :] = hit
                else:
                    side = ix // 2
                    hit = jnp.where(lane == target + 16 * side, 1.0, 0.0).astype(BF16)
                    sel_edge[iz, 32 * c + 16 * side : 32 * c + 16 * side + 16, :] = hit[:, :32]


def build_bands(weight, band, band_t):
    zero = jnp.zeros((C, C), BF16)
    for t in range(9):
        taps = [weight[t // 3, t % 3, e] for e in range(3)]
        for zi in range(4):
            left = taps[zi] if zi < 3 else zero
            right = taps[zi - 1] if zi > 0 else zero
            band[t, C * zi : C * zi + C, :] = jnp.concatenate([left, right], axis=1)
        band_t[8 - t, :C, :] = jnp.concatenate([taps[2], taps[1], taps[0], zero], axis=1)
        band_t[8 - t, C:, :] = jnp.concatenate([zero, taps[2], taps[1], taps[0]], axis=1)


def select(source, choose):
    rows = choose.shape[1]
    low = lax.broadcasted_iota(jnp.int32, (rows, 128), 1) < C
    source = pltpu.roll(source.astype(F32), C, 1).astype(BF16)
    edge = source[:, :128]
    inner = jnp.dot(choose[1], source, preferred_element_type=F32)
    before = jnp.dot(choose[0], edge, preferred_element_type=F32)
    after = jnp.dot(choose[2], edge, preferred_element_type=F32)
    first = jnp.where(low, before, inner[:, :128])
    last = jnp.where(low, inner[:, :128], after)
    return jnp.concatenate([first, inner[:, 128:], last], axis=1).astype(BF16)


def pad_inner(field, raw, sel, padded):
    value = select(raw[field, 1:9].reshape(128, 512), sel)
    for c in range(3):
        start = 160 * c + 16
        padded[field, start : start + 128, :] = value[128 * c : 128 * c + 128]


def pad_edge(field, raw, sel_edge, padded):
    source = jnp.concatenate([raw[field, 0], raw[field, 9]], axis=0)
    value = select(source, sel_edge)
    for c in range(3):
        padded[field, 160 * c : 160 * c + 16, :] = value[32 * c : 32 * c + 16]
        padded[field, 160 * c + 144 : 160 * c + 160, :] = value[32 * c + 16 : 32 * c + 32]


def multiply(part, tap, flipped):
    if flipped:
        return lax.dot_general(part, tap, NT, preferred_element_type=F32)
    return jnp.dot(part, tap, preferred_element_type=F32)


def convolve(padded, field, band, pair, flipped):
    total = None
    for t in range(9):
        start = 160 * (t % 3) + 16 * (t // 3)
        part = padded[field, start : start + 128, 128 * pair : 128 * pair + 256]
        term = multiply(part, band[t], flipped)
        total = term if total is None else total + term
    return total


def convolve_edge(padded, field, band, flipped):
    sides = []
    for layer, a in ((0, 0), (9, 2)):
        total = None
        for c in range(3):
            start = 160 * c + 16 * layer
            part = jnp.concatenate(
                [
                    padded[field, start : start + 16, 128 * pair : 128 * pair + 256]
                    for pair in range(4)
                ],
                axis=0,
            )
            term = multiply(part, band[3 * a + c], flipped)
            total = term if total is None else total + term
        sides.append(total)
    return sides


def filter_taps(t, raw, padded, sums):
    low = lax.broadcasted_iota(jnp.int32, (C, 128), 1) < C
    one = None
    two = None
    at_one = pl.multiple_of(160 * (t % 3) + 16 * (t // 3), 16)
    back = 8 - t
    at_two = pl.multiple_of(160 * (back % 3) + 16 * (back // 3), 16)
    for pair in range(4):
        lanes = slice(128 * pair, 128 * pair + 128)
        wide = slice(128 * pair, 128 * pair + 256)
        ghid = raw[GHID, 1:9, :, lanes].reshape(128, 128)
        middle = raw[MID, 1:9, :, lanes].reshape(128, 128)
        term = lax.dot_general(
            padded[FEAT, pl.ds(at_one, 128), wide], ghid, TN, preferred_element_type=F32
        )
        one = term if one is None else one + term
        term = lax.dot_general(
            middle, padded[GOUT, pl.ds(at_two, 128), wide], TN, preferred_element_type=F32
        )
        two = term if two is None else two + term
    for e in range(3):
        near = one[C * e : C * e + C]
        far = one[C * e + C : C * e + 2 * C]
        pieces = []
        for value, block in ((two[:C], 2 - e), (two[C:], 3 - e)):
            tile = value[:, 128 * (block // 2) : 128 * (block // 2) + 128]
            pieces.append(tile if block % 2 else pltpu.roll(tile, C, 1))
        first_part = near + pltpu.roll(far, C, 1)
        second_part = pieces[0] + pieces[1]
        start = pl.multiple_of(192 * t + C * e, C)
        sums[pl.ds(start, C), :] = jnp.where(low, first_part, second_part)


def kernel(
    ny, nz, scale,
    feat_in, wa_in, wb_in, nb_in, act_in, cot_in,
    out, gfeat, full,
    feat, cot, wa, wb, nb, act,
    raw, sel, sel_edge, padded, band_a, band_at, band_b, band_bt,
    sums, from_core, chip, from_plane, groups,
    in_sem, halo_send, halo_recv, core_send, core_recv, plane_send, plane_recv,
    group_send, group_recv, back_send, back_recv, last_send, last_recv,
):
    count = ny * nz * NCORE
    nhigh = nz // ZLOW
    me = lax.axis_index("dom")
    core = me % NCORE
    z = (me // NCORE) % nz
    y = me // (NCORE * nz)
    zlow = z % ZLOW
    zhigh = z // ZLOW
    spot = y * ZLOW + zlow
    up = (me + 1) % count
    down = (me + count - 1) % count
    partner = me + 1 - 2 * core
    plan = []
    for dy in range(ny - 1, -1, -1):
        for dz in range(ZLOW - 1, -1, -1):
            if dy or dz:
                plan.append((dy, dz))

    def at_plane(step):
        ty = (y + step[0]) % ny
        tz = (zlow + step[1]) % ZLOW
        return ty * ZLOW + tz, (ty * nz + zhigh * ZLOW + tz) * NCORE + core

    def at_group(step):
        return (y * nz + ((zhigh + step) % nhigh) * ZLOW + zlow) * NCORE + core

    raw[:, 0] = jnp.zeros((4, 16, 512), BF16)
    raw[:, 9] = jnp.zeros((4, 16, 512), BF16)
    barrier = pltpu.get_barrier_semaphore()
    pl.semaphore_signal(barrier, inc=1, device_id={"dom": up})
    pl.semaphore_signal(barrier, inc=1, device_id={"dom": down})
    for step in plan:
        pl.semaphore_signal(barrier, inc=1, device_id={"dom": at_plane(step)[1]})
    for step in range(1, nhigh):
        pl.semaphore_signal(barrier, inc=1, device_id={"dom": at_group(step)})

    loads = [
        pltpu.make_async_copy(source, target, in_sem.at[i])
        for i, (source, target) in enumerate(
            ((nb_in, nb), (act_in, act), (feat_in, feat), (cot_in, cot), (wa_in, wa), (wb_in, wb))
        )
    ]
    for load in loads:
        load.start()
    for field in (FEAT, GOUT):
        for c in range(3):
            padded[field, 160 * c : 160 * c + 16, :] = jnp.zeros((16, 640), BF16)
            padded[field, 160 * c + 144 : 160 * c + 160, :] = jnp.zeros((16, 640), BF16)
    chip[HALF:, :] = jnp.zeros((CH * ny * ZLOW - HALF, 128), BF16)
    for load in loads[:4]:
        load.wait()
    keep = [jnp.where(act[b] > 0, 1.0, 0.0) for b in range(2)]
    rows = lax.broadcasted_iota(jnp.int32, (128, 128), 0)
    alive = jnp.where((rows & 8) == 0, keep[0], keep[1])
    raw[FEAT, 1:9] = jnp.concatenate(
        [feat[b].astype(F32) for b in range(2)], axis=1
    ).astype(BF16)
    raw[GOUT, 1:9] = jnp.concatenate(
        [cot[b].astype(F32) * keep[b] for b in range(2)], axis=1
    ).astype(BF16)

    def halo(number):
        fields = slice(2 * number, 2 * number + 2)
        return [
            pltpu.make_async_remote_copy(
                src_ref=raw.at[fields, source],
                dst_ref=raw.at[fields, target],
                send_sem=halo_send.at[2 * number + way],
                recv_sem=halo_recv.at[2 * number + way],
                device_id={"dom": device},
            )
            for way, (source, target, device) in enumerate(((8, 0, up), (1, 9, down)))
        ]

    def halo_start(copies):
        @pl.when(me < count - 1)
        def _():
            copies[0].start()

        @pl.when(me > 0)
        def _():
            copies[1].start()

    def halo_wait(copies):
        @pl.when(me < count - 1)
        def _():
            copies[0].wait_send()
            copies[1].wait_recv()

        @pl.when(me > 0)
        def _():
            copies[1].wait_send()
            copies[0].wait_recv()

    pl.semaphore_wait(barrier, 2 + len(plan) + nhigh - 1)
    first = halo(0)
    halo_start(first)
    build_selection(nb, sel, sel_edge)
    pad_inner(FEAT, raw, sel, padded)
    pad_inner(GOUT, raw, sel, padded)
    for load in loads[4:]:
        load.wait()
    build_bands(wa, band_a, band_at)
    build_bands(wb, band_b, band_bt)
    hidden = [convolve(padded, FEAT, band_a, pair, False) for pair in range(4)]
    grad = [convolve(padded, GOUT, band_bt, pair, True) for pair in range(4)]
    halo_wait(first)
    pad_edge(FEAT, raw, sel_edge, padded)
    pad_edge(GOUT, raw, sel_edge, padded)
    hidden_edge = convolve_edge(padded, FEAT, band_a, False)
    grad_edge = convolve_edge(padded, GOUT, band_bt, True)
    for pair in range(4):
        lanes = slice(128 * pair, 128 * pair + 128)
        some = slice(16 * pair, 16 * pair + 16)

        def joined(value, sides):
            return jnp.concatenate(
                [value[:16] + sides[0][some], value[16:112], value[112:] + sides[1][some]], axis=0
            )

        h = joined(hidden[pair], hidden_edge)
        g = joined(grad[pair], grad_edge)
        s = jax.nn.sigmoid(h)
        middle = alive * (h * s)
        ghid = g * (s * (1.0 + h * (1.0 - s)))
        raw[MID, 1:9, :, lanes] = middle.astype(BF16).reshape(8, 16, 128)
        raw[GHID, 1:9, :, lanes] = ghid.astype(BF16).reshape(8, 16, 128)
    second = halo(1)
    halo_start(second)

    for i in range(5):
        filter_taps(4 * (1 - core) + i, raw, padded, sums)
    own = pl.multiple_of(core * HALF, 8)
    other = pl.multiple_of((1 - core) * HALF, 8)
    to_core = pltpu.make_async_remote_copy(
        src_ref=sums.at[pl.ds(other, HALF)],
        dst_ref=from_core,
        send_sem=core_send,
        recv_sem=core_recv,
        device_id={"dom": partner},
    )
    to_core.start()
    for i in range(4):
        filter_taps(5 * core + i, raw, padded, sums)
    to_core.wait_recv()
    from_core[...] = from_core[...] + sums[pl.ds(own, HALF), :]
    chip[:HALF, :] = from_core[...].astype(BF16)

    to_plane = []
    for i, step in enumerate(plan):
        spot_to, device = at_plane(step)
        begin = pl.multiple_of(spot_to * CH, CH)
        to_plane.append(
            pltpu.make_async_remote_copy(
                src_ref=chip.at[pl.ds(begin, CH)],
                dst_ref=from_plane.at[i],
                send_sem=plane_send.at[i],
                recv_sem=plane_recv.at[i],
                device_id={"dom": device},
            )
        )
    for copy in to_plane:
        copy.start()

    def last(field, band, flipped, target, base, masked):
        for pair in range(4):
            lanes = slice(128 * pair, 128 * pair + 128)
            value = convolve(padded, field, band, pair, flipped)
            if masked:
                value = value * alive
            value = value.reshape(8, 16, 128)
            for b in range(2):
                given = base[b, :, :, lanes].astype(F32)
                if masked:
                    given = given * keep[b]
                target[b, :, :, lanes] = (given + value[:, 8 * b : 8 * b + 8]).astype(BF16)

    halo_wait(second)
    for field in (MID, GHID):
        pad_inner(field, raw, sel, padded)
        pad_edge(field, raw, sel_edge, padded)
    last(MID, band_b, False, out, feat, False)

    total = chip[pl.ds(pl.multiple_of(spot * CH, CH), CH), :].astype(F32)
    for copy in to_plane:
        copy.wait_recv()
    for i in range(len(plan)):
        total = total + from_plane[i].astype(F32)
    groups[zhigh] = total
    to_group = [
        pltpu.make_async_remote_copy(
            src_ref=groups.at[zhigh],
            dst_ref=groups.at[zhigh],
            send_sem=group_send.at[step - 1],
            recv_sem=group_recv.at[step - 1],
            device_id={"dom": at_group(step)},
        )
        for step in range(1, nhigh)
    ]
    for copy in to_group:
        copy.start()
    last(GHID, band_at, True, gfeat, cot, True)
    for copy in to_group:
        copy.wait_recv()
    total = groups[0]
    for i in range(1, nhigh):
        total = total + groups[i]
    full[core, spot] = (total * scale).astype(BF16)
    back = [
        pltpu.make_async_remote_copy(
            src_ref=full.at[core, spot],
            dst_ref=full.at[core, spot],
            send_sem=back_send.at[i],
            recv_sem=back_recv.at[i],
            device_id={"dom": at_plane(step)[1]},
        )
        for i, step in enumerate(plan)
    ]
    for copy in back:
        copy.start()
    to_core.wait_send()
    for copy in to_plane + to_group:
        copy.wait_send()
    for copy in back:
        copy.wait_recv()
    to_last = pltpu.make_async_remote_copy(
        src_ref=full.at[core],
        dst_ref=full.at[core],
        send_sem=last_send,
        recv_sem=last_recv,
        device_id={"dom": partner},
    )
    to_last.start()
    for copy in back:
        copy.wait_send()
    to_last.wait()


def finish(out_in, gfeat_in, full, out, gfeat, fa, fb, fa_here, fb_here, sems):
    copies = [
        pltpu.make_async_copy(source, target, sems.at[i])
        for i, (source, target) in enumerate(
            ((out_in, out), (gfeat_in, gfeat), (fa_here, fa), (fb_here, fb))
        )
    ]
    copies[0].start()
    copies[1].start()
    for h in range(NCORE):
        value = full[h].reshape(full.shape[1] * CH, 128)[:HALF].astype(F32)
        fa_here[h * HALF : h * HALF + HALF, :] = value[:, :C]
        fb_here[h * HALF : h * HALF + HALF, :] = pltpu.roll(value, C, 1)[:, :C]
    copies[2].start()
    copies[3].start()
    for copy in copies:
        copy.wait()


def on_device(ny, nz, features, weight_first, weight_second, neighbours, active, cotangent):
    count = ny * nz * NCORE
    scale = 1.0 / math.sqrt(2 * count * E**3)
    plane = ny * ZLOW
    nhigh = nz // ZLOW
    vmem = pl.BlockSpec(memory_space=pltpu.VMEM)
    hbm = pl.BlockSpec(memory_space=pltpu.HBM)
    dma = pltpu.SemaphoreType.DMA
    brick = jax.ShapeDtypeStruct(features.shape, BF16)
    out, gfeat, full = pl.pallas_call(
        functools.partial(kernel, ny, nz, scale),
        out_shape=(brick, brick, jax.ShapeDtypeStruct((NCORE, plane, CH, 128), BF16)),
        in_specs=[hbm] * 6,
        out_specs=(vmem, vmem, vmem),
        scratch_shapes=[
            pltpu.VMEM(features.shape, BF16),
            pltpu.VMEM(features.shape, BF16),
            pltpu.VMEM(weight_first.shape, BF16),
            pltpu.VMEM(weight_first.shape, BF16),
            pltpu.SMEM(neighbours.shape, jnp.int32),
            pltpu.SMEM(active.shape, jnp.int32),
            pltpu.VMEM((4, 10, 16, 512), BF16),
            pltpu.VMEM((3, 384, 128), BF16),
            pltpu.VMEM((3, 96, 32), BF16),
            pltpu.VMEM((4, 480, 640), BF16),
            pltpu.VMEM((9, 256, 128), BF16),
            pltpu.VMEM((9, 128, 256), BF16),
            pltpu.VMEM((9, 256, 128), BF16),
            pltpu.VMEM((9, 128, 256), BF16),
            pltpu.VMEM((ROWS, 128), F32),
            pltpu.VMEM((HALF, 128), F32),
            pltpu.VMEM((plane * CH, 128), BF16),
            pltpu.VMEM((plane - 1, CH, 128), BF16),
            pltpu.VMEM((nhigh, CH, 128), F32),
            dma((6,)),
            dma((4,)), dma((4,)),
            dma, dma,
            dma((plane - 1,)), dma((plane - 1,)),
            dma((nhigh - 1,)), dma((nhigh - 1,)),
            dma((plane - 1,)), dma((plane - 1,)),
            dma, dma,
        ],
        compiler_params=pltpu.CompilerParams(
            collective_id=0, has_side_effects=True, vmem_limit_bytes=48 * 2**20
        ),
    )(
        *[
            pltpu.with_memory_space_constraint(value, pltpu.HBM)
            for value in (
                features, weight_first, weight_second, neighbours, active, cotangent
            )
        ]
    )
    grads = jax.ShapeDtypeStruct((ROWS, C), F32)
    out, gfeat, fa, fb = pl.pallas_call(
        finish,
        out_shape=(brick, brick, grads, grads),
        in_specs=[vmem] * 3,
        out_specs=(hbm,) * 4,
        scratch_shapes=[pltpu.VMEM((ROWS, C), F32), pltpu.VMEM((ROWS, C), F32), dma((4,))],
        compiler_params=pltpu.CompilerParams(vmem_limit_bytes=24 * 2**20),
    )(out, gfeat, full)
    return out, gfeat, fa.reshape(3, 3, 3, C, C), fb.reshape(3, 3, 3, C, C)


def solution(mesh):
    count = mesh.shape["dom"]
    return jax.shard_map(
        functools.partial(on_device, count // (NZ * NCORE), NZ),
        mesh=mesh,
        in_specs=(
            P(("scene", "dom"), None, None, None),
            P(),
            P(),
            P(("scene", "dom"), None),
            P(("scene", "dom")),
            P(("scene", "dom"), None, None, None),
        ),
        out_specs=(
            P(("scene", "dom"), None, None, None),
            P(("scene", "dom"), None, None, None),
            P("scene", None, None, None, None),
            P("scene", None, None, None, None),
        ),
        check_vma=False,
    )
```

```python
import functools
import math

import jax
import jax.numpy as jnp
from jax import lax
from jax.experimental import pallas as pl
from jax.experimental.pallas import tpu as pltpu
from jax.sharding import PartitionSpec as P

C = 64
E = 8
FEAT, GOUT = 0, 1
MID, GHID = 0, 1
TN = (((0,), (0,)), ((), ()))
NT = (((1,), (1,)), ((), ()))
ROWS = 27 * C
HALF = ROWS // 2
NCORE = 2
NZ = 16
ZLOW = 4
CH = 64
F32 = jnp.float32
BF16 = jnp.bfloat16


def entry(nb, brick, offset):
    if offset == (0, 0, 0):
        return 8 * brick
    place = (offset[0] + 1) * 9 + (offset[1] + 1) * 3 + offset[2] + 1
    ident = nb[brick, place if place < 13 else place - 1]
    return jnp.where(ident < 0, -1000, (ident & 1) * 8)


def build_selection(nb, sel, sel_edge):
    row = lax.broadcasted_iota(jnp.int32, (16, 128), 0)
    lane = lax.broadcasted_iota(jnp.int32, (16, 128), 1)
    y = row & 7
    second = row >= 8
    for iz in range(3):
        for c in range(3):
            yy = y + (c - 1)
            wrap = (yy < 0) | (yy > 7)
            for ix in range(3):
                codes = []
                for brick in range(2):
                    inner = entry(nb, brick, (ix - 1, 0, iz - 1))
                    if c == 1:
                        codes.append(jnp.full((16, 128), inner, jnp.int32))
                    else:
                        outer = entry(nb, brick, (ix - 1, c - 1, iz - 1))
                        codes.append(jnp.where(wrap, outer, inner))
                target = jnp.where(second, codes[1], codes[0]) + (yy & 7)
                if ix == 1:
                    for x in range(8):
                        hit = jnp.where(lane == target + 16 * x, 1.0, 0.0).astype(BF16)
                        sel[iz, 128 * c + 16 * x : 128 * c + 16 * x + 16, :] = hit
                else:
                    side = ix // 2
                    hit = jnp.where(lane == target + 16 * side, 1.0, 0.0).astype(BF16)
                    sel_edge[iz, 32 * c + 16 * side : 32 * c + 16 * side + 16, :] = hit[:, :32]


def build_bands(weight, band, band_t):
    zero = jnp.zeros((C, C), BF16)
    for t in range(9):
        taps = [weight[t // 3, t % 3, e] for e in range(3)]
        for zi in range(4):
            left = taps[zi] if zi < 3 else zero
            right = taps[zi - 1] if zi > 0 else zero
            band[t, C * zi : C * zi + C, :] = jnp.concatenate([left, right], axis=1)
        band_t[8 - t, :C, :] = jnp.concatenate([taps[2], taps[1], taps[0], zero], axis=1)
        band_t[8 - t, C:, :] = jnp.concatenate([zero, taps[2], taps[1], taps[0]], axis=1)


def select(source, choose):
    rows = choose.shape[1]
    low = lax.broadcasted_iota(jnp.int32, (rows, 128), 1) < C
    source = pltpu.roll(source.astype(F32), C, 1).astype(BF16)
    edge = source[:, :128]
    inner = jnp.dot(choose[1], source, preferred_element_type=F32)
    before = jnp.dot(choose[0], edge, preferred_element_type=F32)
    after = jnp.dot(choose[2], edge, preferred_element_type=F32)
    first = jnp.where(low, before, inner[:, :128])
    last = jnp.where(low, inner[:, :128], after)
    return jnp.concatenate([first, inner[:, 128:], last], axis=1).astype(BF16)


def pad_inner(layers, sel, padded, field):
    value = select(layers.reshape(128, 512), sel)
    for c in range(3):
        start = 160 * c + 16
        padded[field, start : start + 128, :] = value[128 * c : 128 * c + 128]


def pad_edge(below, above, sel_edge, padded, field):
    value = select(jnp.concatenate([below, above], axis=0), sel_edge)
    for c in range(3):
        padded[field, 160 * c : 160 * c + 16, :] = value[32 * c : 32 * c + 16]
        padded[field, 160 * c + 144 : 160 * c + 160, :] = value[32 * c + 16 : 32 * c + 32]


def multiply(part, tap, flipped):
    if flipped:
        return lax.dot_general(part, tap, NT, preferred_element_type=F32)
    return jnp.dot(part, tap, preferred_element_type=F32)


def convolve(padded, field, band, pair, flipped):
    total = None
    for t in range(9):
        start = 160 * (t % 3) + 16 * (t // 3)
        part = padded[field, start : start + 128, 128 * pair : 128 * pair + 256]
        term = multiply(part, band[t], flipped)
        total = term if total is None else total + term
    return total


def filter_taps(t, late, padded, sums):
    low = lax.broadcasted_iota(jnp.int32, (C, 128), 1) < C
    one = None
    two = None
    at_one = pl.multiple_of(160 * (t % 3) + 16 * (t // 3), 16)
    back = 8 - t
    at_two = pl.multiple_of(160 * (back % 3) + 16 * (back // 3), 16)
    for pair in range(4):
        lanes = slice(128 * pair, 128 * pair + 128)
        wide = slice(128 * pair, 128 * pair + 256)
        ghid = late[GHID, 1:9, :, lanes].reshape(128, 128)
        middle = late[MID, 1:9, :, lanes].reshape(128, 128)
        term = lax.dot_general(
            padded[FEAT, pl.ds(at_one, 128), wide], ghid, TN, preferred_element_type=F32
        )
        one = term if one is None else one + term
        term = lax.dot_general(
            middle, padded[GOUT, pl.ds(at_two, 128), wide], TN, preferred_element_type=F32
        )
        two = term if two is None else two + term
    for e in range(3):
        near = one[C * e : C * e + C]
        far = one[C * e + C : C * e + 2 * C]
        pieces = []
        for value, block in ((two[:C], 2 - e), (two[C:], 3 - e)):
            tile = value[:, 128 * (block // 2) : 128 * (block // 2) + 128]
            pieces.append(tile if block % 2 else pltpu.roll(tile, C, 1))
        first_part = near + pltpu.roll(far, C, 1)
        second_part = pieces[0] + pieces[1]
        start = pl.multiple_of(192 * t + C * e, C)
        sums[pl.ds(start, C), :] = jnp.where(low, first_part, second_part)


def halo_copies(layers, send, recv, count, me):
    up = (me + 1) % count
    down = (me + count - 1) % count
    return [
        pltpu.make_async_remote_copy(
            src_ref=layers.at[:, source],
            dst_ref=layers.at[:, target],
            send_sem=send.at[way],
            recv_sem=recv.at[way],
            device_id={"dom": device},
        )
        for way, (source, target, device) in enumerate(((8, 0, up), (1, 9, down)))
    ]


def halo_start(copies, count, me):
    @pl.when(me < count - 1)
    def _():
        copies[0].start()

    @pl.when(me > 0)
    def _():
        copies[1].start()


def halo_wait(copies, count, me):
    @pl.when(me < count - 1)
    def _():
        copies[0].wait_send()
        copies[1].wait_recv()

    @pl.when(me > 0)
    def _():
        copies[1].wait_send()
        copies[0].wait_recv()


def prepare(
    count,
    feat_in, wa_in, wb_in, nb_in, act_in, cot_in,
    given, padded, sel, sel_edge, band_a, band_at, band_b, band_bt, alive,
    feat, cot, wa, wb, nb, act, raw,
    in_sem, halo_send, halo_recv,
):
    me = lax.axis_index("dom")
    raw[:, 0] = jnp.zeros((2, 16, 512), BF16)
    raw[:, 9] = jnp.zeros((2, 16, 512), BF16)
    barrier = pltpu.get_barrier_semaphore()
    pl.semaphore_signal(barrier, inc=1, device_id={"dom": (me + 1) % count})
    pl.semaphore_signal(barrier, inc=1, device_id={"dom": (me + count - 1) % count})
    loads = [
        pltpu.make_async_copy(source, target, in_sem.at[i])
        for i, (source, target) in enumerate(
            ((act_in, act), (feat_in, feat), (cot_in, cot), (nb_in, nb), (wa_in, wa), (wb_in, wb))
        )
    ]
    for load in loads:
        load.start()
    for load in loads[:3]:
        load.wait()
    keep = [jnp.where(act[b] > 0, 1.0, 0.0) for b in range(2)]
    raw[FEAT, 1:9] = jnp.concatenate(
        [feat[b].astype(F32) for b in range(2)], axis=1
    ).astype(BF16)
    raw[GOUT, 1:9] = jnp.concatenate(
        [cot[b].astype(F32) * keep[b] for b in range(2)], axis=1
    ).astype(BF16)
    pl.semaphore_wait(barrier, 2)
    halo = halo_copies(raw, halo_send, halo_recv, count, me)
    halo_start(halo, count, me)
    given[...] = raw[:, 1:9]
    rows = lax.broadcasted_iota(jnp.int32, (128, 128), 0)
    alive[...] = jnp.where((rows & 8) == 0, keep[0], keep[1])
    for load in loads[3:]:
        load.wait()
    build_selection(nb, sel, sel_edge)
    for field in (FEAT, GOUT):
        pad_inner(raw[field, 1:9], sel, padded, field)
    build_bands(wa, band_a, band_at)
    build_bands(wb, band_b, band_bt)
    halo_wait(halo, count, me)
    for field in (FEAT, GOUT):
        pad_edge(raw[field, 0], raw[field, 9], sel_edge, padded, field)


def kernel(
    ny, nz, scale,
    given, padded, sel, sel_edge, band_a, band_at, band_b, band_bt, alive,
    out, gfeat, full,
    late, late_padded, sums, from_core, chip, from_plane, groups,
    halo_send, halo_recv, core_send, core_recv, plane_send, plane_recv,
    group_send, group_recv, back_send, back_recv, last_send, last_recv,
):
    count = ny * nz * NCORE
    plane = ny * ZLOW
    nhigh = nz // ZLOW
    live = -(-HALF // CH)
    me = lax.axis_index("dom")
    core = me % NCORE
    y = me // (NCORE * nz)
    shift = (ZLOW // 2) * core
    z = ((me // NCORE) % nz + shift) % nz
    zlow = z % ZLOW
    zhigh = z // ZLOW
    spot = y * ZLOW + zlow
    partner = me + 1 - 2 * core
    order = sorted(
        range(1, plane),
        key=lambda step: (0, 1, 2, 1)[step // ZLOW] + (0, 1, 2, 2)[step % ZLOW],
        reverse=True,
    )

    def device_at(ty, tz):
        return (ty * nz + (tz + nz - shift) % nz) * NCORE + core

    def at_plane(step):
        return device_at((spot ^ step) // ZLOW, zhigh * ZLOW + (spot ^ step) % ZLOW)

    def at_group(step):
        return device_at(y, ((zhigh + step) % nhigh) * ZLOW + zlow)

    late[:, 0] = jnp.zeros((2, 16, 512), BF16)
    late[:, 9] = jnp.zeros((2, 16, 512), BF16)
    barrier = pltpu.get_barrier_semaphore()
    for step in range(1, nhigh):
        pl.semaphore_signal(barrier, inc=1, device_id={"dom": at_group(step)})
    for step in order:
        pl.semaphore_signal(barrier, inc=1, device_id={"dom": at_plane(step)})
    pl.semaphore_signal(barrier, inc=1, device_id={"dom": (me + 1) % count})
    pl.semaphore_signal(barrier, inc=1, device_id={"dom": (me + count - 1) % count})

    chip[HALF:, :] = jnp.zeros((CH * plane - HALF, 128), BF16)
    for pair in range(4):
        lanes = slice(128 * pair, 128 * pair + 128)
        h = convolve(padded, FEAT, band_a, pair, False)
        g = convolve(padded, GOUT, band_bt, pair, True)
        s = jax.nn.sigmoid(h)
        middle = alive[...] * (h * s)
        ghid = g * (s * (1.0 + h * (1.0 - s)))
        late[MID, 1:9, :, lanes] = middle.astype(BF16).reshape(8, 16, 128)
        late[GHID, 1:9, :, lanes] = ghid.astype(BF16).reshape(8, 16, 128)
    for i in range(5):
        filter_taps(4 * (1 - core) + i, late, padded, sums)
    pl.semaphore_wait(barrier, 2 + plane - 1 + nhigh - 1)

    own = pl.multiple_of(core * HALF, 8)
    other = pl.multiple_of((1 - core) * HALF, 8)
    to_core = pltpu.make_async_remote_copy(
        src_ref=sums.at[pl.ds(other, HALF)],
        dst_ref=from_core,
        send_sem=core_send,
        recv_sem=core_recv,
        device_id={"dom": partner},
    )
    to_core.start()
    halo = halo_copies(late, halo_send, halo_recv, count, me)
    halo_start(halo, count, me)
    for i in range(4):
        filter_taps(5 * core + i, late, padded, sums)
    to_core.wait_recv()
    from_core[...] = from_core[...] + sums[pl.ds(own, HALF), :]
    chip[:HALF, :] = from_core[...].astype(BF16)

    def plane_copy(step):
        return pltpu.make_async_remote_copy(
            src_ref=chip.at[pl.ds(pl.multiple_of((spot ^ step) * CH, CH), CH)],
            dst_ref=from_plane.at[step - 1],
            send_sem=plane_send.at[step - 1],
            recv_sem=plane_recv.at[step - 1],
            device_id={"dom": at_plane(step)},
        )

    for step in order:

        @pl.when((spot ^ step) < live)
        def _():
            plane_copy(step).start()

    def last(field, band, flipped, target, base):
        for pair in range(4):
            lanes = slice(128 * pair, 128 * pair + 128)
            value = convolve(late_padded, field, band, pair, flipped)
            if flipped:
                value = value * alive[...]
            value = value.reshape(8, 16, 128) + given[base, :, :, lanes].astype(F32)
            for b in range(2):
                target[b, :, :, lanes] = value[:, 8 * b : 8 * b + 8].astype(BF16)

    halo_wait(halo, count, me)
    for field in (MID, GHID):
        pad_inner(late[field, 1:9], sel, late_padded, field)
        pad_edge(late[field, 0], late[field, 9], sel_edge, late_padded, field)
    last(MID, band_b, False, out, FEAT)

    to_group = [
        pltpu.make_async_remote_copy(
            src_ref=groups.at[zhigh],
            dst_ref=groups.at[zhigh],
            send_sem=group_send.at[step - 1],
            recv_sem=group_recv.at[step - 1],
            device_id={"dom": at_group(step)},
        )
        for step in range(1, nhigh)
    ]
    back = {
        step: pltpu.make_async_remote_copy(
            src_ref=full.at[core, spot],
            dst_ref=full.at[core, spot],
            send_sem=back_send.at[step - 1],
            recv_sem=back_recv.at[step - 1],
            device_id={"dom": at_plane(step)},
        )
        for step in order
    }

    def forward(place):
        return pltpu.make_async_remote_copy(
            src_ref=full.at[core, place],
            dst_ref=full.at[core, place],
            send_sem=last_send.at[place],
            recv_sem=last_recv.at[place],
            device_id={"dom": partner},
        )

    @pl.when(spot < live)
    def _():
        total = chip[pl.ds(pl.multiple_of(spot * CH, CH), CH), :].astype(F32)
        for step in order:
            plane_copy(step).wait_recv()
        for step in range(1, plane):
            total = total + from_plane[step - 1].astype(F32)
        groups[zhigh] = total.astype(BF16)
        for copy in to_group:
            copy.start()

    last(GHID, band_at, True, gfeat, GOUT)

    @pl.when(spot < live)
    def _():
        for copy in to_group:
            copy.wait_recv()
        total = groups[0].astype(F32)
        for i in range(1, nhigh):
            total = total + groups[i].astype(F32)
        full[core, spot] = (total * scale).astype(BF16)
        for step in order:
            back[step].start()
        forward(spot).start()

    to_core.wait_send()
    for step in order:

        @pl.when((spot ^ step) < live)
        def _():
            plane_copy(step).wait_send()

    for step in order[::-1]:

        @pl.when((spot ^ step) < live)
        def _():
            back[step].wait_recv()
            forward(spot ^ step).start()

    @pl.when(spot < live)
    def _():
        for copy in to_group:
            copy.wait_send()
        for step in order:
            back[step].wait_send()

    for place in range(live):
        forward(place).wait()


def finish(out_in, gfeat_in, full, out, gfeat, fa, fb, fa_here, fb_here, sems):
    copies = [
        pltpu.make_async_copy(out_in, out, sems.at[0]),
        pltpu.make_async_copy(gfeat_in, gfeat, sems.at[1]),
    ]
    for copy in copies:
        copy.start()
    for h in range(NCORE):
        rows = slice(h * HALF, h * HALF + HALF)
        value = full[h].reshape(full.shape[1] * CH, 128)[:HALF].astype(F32)
        fa_here[rows, :] = value[:, :C]
        fb_here[rows, :] = pltpu.roll(value, C, 1)[:, :C]
        for i, (here, there) in enumerate(((fa_here, fa), (fb_here, fb))):
            copy = pltpu.make_async_copy(here.at[rows], there.at[rows], sems.at[2 + 2 * h + i])
            copy.start()
            copies.append(copy)
    for copy in copies:
        copy.wait()


def on_device(ny, nz, features, weight_first, weight_second, neighbours, active, cotangent):
    count = ny * nz * NCORE
    scale = 1.0 / math.sqrt(2 * count * E**3)
    plane = ny * ZLOW
    nhigh = nz // ZLOW
    vmem = pl.BlockSpec(memory_space=pltpu.VMEM)
    hbm = pl.BlockSpec(memory_space=pltpu.HBM)
    dma = pltpu.SemaphoreType.DMA
    brick = jax.ShapeDtypeStruct(features.shape, BF16)
    whole = pltpu.VMEM(features.shape, BF16)
    taps = pltpu.VMEM(weight_first.shape, BF16)
    prepared = pl.pallas_call(
        functools.partial(prepare, count),
        out_shape=(
            jax.ShapeDtypeStruct((2, 8, 16, 512), BF16),
            jax.ShapeDtypeStruct((2, 480, 640), BF16),
            jax.ShapeDtypeStruct((3, 384, 128), BF16),
            jax.ShapeDtypeStruct((3, 96, 32), BF16),
            jax.ShapeDtypeStruct((9, 256, 128), BF16),
            jax.ShapeDtypeStruct((9, 128, 256), BF16),
            jax.ShapeDtypeStruct((9, 256, 128), BF16),
            jax.ShapeDtypeStruct((9, 128, 256), BF16),
            jax.ShapeDtypeStruct((128, 128), F32),
        ),
        in_specs=[hbm] * 6,
        out_specs=(vmem,) * 9,
        scratch_shapes=[
            whole, whole, taps, taps,
            pltpu.SMEM(neighbours.shape, jnp.int32),
            pltpu.SMEM(active.shape, jnp.int32),
            pltpu.VMEM((2, 10, 16, 512), BF16),
            dma((6,)), dma((2,)), dma((2,)),
        ],
        compiler_params=pltpu.CompilerParams(
            collective_id=0, has_side_effects=True, vmem_limit_bytes=24 * 2**20
        ),
    )(
        *[
            pltpu.with_memory_space_constraint(value, pltpu.HBM)
            for value in (
                features, weight_first, weight_second, neighbours, active, cotangent
            )
        ]
    )
    out, gfeat, full = pl.pallas_call(
        functools.partial(kernel, ny, nz, scale),
        out_shape=(brick, brick, jax.ShapeDtypeStruct((NCORE, plane, CH, 128), BF16)),
        in_specs=[vmem] * 9,
        out_specs=(vmem, vmem, vmem),
        scratch_shapes=[
            pltpu.VMEM((2, 10, 16, 512), BF16),
            pltpu.VMEM((2, 480, 640), BF16),
            pltpu.VMEM((ROWS, 128), F32),
            pltpu.VMEM((HALF, 128), F32),
            pltpu.VMEM((plane * CH, 128), BF16),
            pltpu.VMEM((plane - 1, CH, 128), BF16),
            pltpu.VMEM((nhigh, CH, 128), BF16),
            dma((2,)), dma((2,)),
            dma, dma,
            dma((plane - 1,)), dma((plane - 1,)),
            dma((nhigh - 1,)), dma((nhigh - 1,)),
            dma((plane - 1,)), dma((plane - 1,)),
            dma((plane,)), dma((plane,)),
        ],
        compiler_params=pltpu.CompilerParams(
            collective_id=1, has_side_effects=True, vmem_limit_bytes=24 * 2**20
        ),
    )(*prepared)
    grads = jax.ShapeDtypeStruct((ROWS, C), F32)
    out, gfeat, fa, fb = pl.pallas_call(
        finish,
        out_shape=(brick, brick, grads, grads),
        in_specs=[vmem] * 3,
        out_specs=(hbm,) * 4,
        scratch_shapes=[pltpu.VMEM((ROWS, C), F32), pltpu.VMEM((ROWS, C), F32), dma((6,))],
        compiler_params=pltpu.CompilerParams(vmem_limit_bytes=24 * 2**20),
    )(out, gfeat, full)
    return out, gfeat, fa.reshape(3, 3, 3, C, C), fb.reshape(3, 3, 3, C, C)


def solution(mesh):
    count = mesh.shape["dom"]
    return jax.shard_map(
        functools.partial(on_device, count // (NZ * NCORE), NZ),
        mesh=mesh,
        in_specs=(
            P(("scene", "dom"), None, None, None),
            P(),
            P(),
            P(("scene", "dom"), None),
            P(("scene", "dom")),
            P(("scene", "dom"), None, None, None),
        ),
        out_specs=(
            P(("scene", "dom"), None, None, None),
            P(("scene", "dom"), None, None, None),
            P("scene", None, None, None, None),
            P("scene", None, None, None, None),
        ),
        check_vma=False,
    )
```

```python
import functools
import math

import jax
import jax.numpy as jnp
from jax import lax
from jax.experimental import pallas as pl
from jax.experimental.pallas import tpu as pltpu
from jax.sharding import PartitionSpec as P

C = 64
E = 8
FEAT, GOUT = 0, 1
MID, GHID = 0, 1
TN = (((0,), (0,)), ((), ()))
NT = (((1,), (1,)), ((), ()))
ROWS = 27 * C
HALF = ROWS // 2
NCORE = 2
NZ = 16
ZLOW = 4
CH = 64
F32 = jnp.float32
BF16 = jnp.bfloat16


def entry(nb, brick, offset):
    if offset == (0, 0, 0):
        return 8 * brick
    place = (offset[0] + 1) * 9 + (offset[1] + 1) * 3 + offset[2] + 1
    ident = nb[brick, place if place < 13 else place - 1]
    return jnp.where(ident < 0, -1000, (ident & 1) * 8)


def build_selection(nb, sel, sel_edge):
    row = lax.broadcasted_iota(jnp.int32, (16, 128), 0)
    lane = lax.broadcasted_iota(jnp.int32, (16, 128), 1)
    y = row & 7
    second = row >= 8
    for iz in range(3):
        for c in range(3):
            yy = y + (c - 1)
            wrap = (yy < 0) | (yy > 7)
            for ix in range(3):
                codes = []
                for brick in range(2):
                    inner = entry(nb, brick, (ix - 1, 0, iz - 1))
                    if c == 1:
                        codes.append(jnp.full((16, 128), inner, jnp.int32))
                    else:
                        outer = entry(nb, brick, (ix - 1, c - 1, iz - 1))
                        codes.append(jnp.where(wrap, outer, inner))
                target = jnp.where(second, codes[1], codes[0]) + (yy & 7)
                if ix == 1:
                    for x in range(8):
                        hit = jnp.where(lane == target + 16 * x, 1.0, 0.0).astype(BF16)
                        sel[iz, 128 * c + 16 * x : 128 * c + 16 * x + 16, :] = hit
                else:
                    side = ix // 2
                    hit = jnp.where(lane == target + 16 * side, 1.0, 0.0).astype(BF16)
                    sel_edge[iz, 32 * c + 16 * side : 32 * c + 16 * side + 16, :] = hit[:, :32]


def build_bands(weight, band, band_t):
    zero = jnp.zeros((C, C), BF16)
    for t in range(9):
        taps = [weight[t // 3, t % 3, e] for e in range(3)]
        for zi in range(4):
            left = taps[zi] if zi < 3 else zero
            right = taps[zi - 1] if zi > 0 else zero
            band[t, C * zi : C * zi + C, :] = jnp.concatenate([left, right], axis=1)
        band_t[8 - t, :C, :] = jnp.concatenate([taps[2], taps[1], taps[0], zero], axis=1)
        band_t[8 - t, C:, :] = jnp.concatenate([zero, taps[2], taps[1], taps[0]], axis=1)


def select(source, choose):
    rows = choose.shape[1]
    low = lax.broadcasted_iota(jnp.int32, (rows, 128), 1) < C
    source = pltpu.roll(source.astype(F32), C, 1).astype(BF16)
    edge = source[:, :128]
    inner = jnp.dot(choose[1], source, preferred_element_type=F32)
    before = jnp.dot(choose[0], edge, preferred_element_type=F32)
    after = jnp.dot(choose[2], edge, preferred_element_type=F32)
    first = jnp.where(low, before, inner[:, :128])
    last = jnp.where(low, inner[:, :128], after)
    return jnp.concatenate([first, inner[:, 128:], last], axis=1).astype(BF16)


def pad_inner(layers, sel, padded, field):
    value = select(layers.reshape(128, 512), sel)
    for c in range(3):
        start = 160 * c + 16
        padded[field, start : start + 128, :] = value[128 * c : 128 * c + 128]


def pad_edge(below, above, sel_edge, padded, field):
    value = select(jnp.concatenate([below, above], axis=0), sel_edge)
    for c in range(3):
        padded[field, 160 * c : 160 * c + 16, :] = value[32 * c : 32 * c + 16]
        padded[field, 160 * c + 144 : 160 * c + 160, :] = value[32 * c + 16 : 32 * c + 32]


def multiply(part, tap, flipped):
    if flipped:
        return lax.dot_general(part, tap, NT, preferred_element_type=F32)
    return jnp.dot(part, tap, preferred_element_type=F32)


def convolve(padded, field, band, pair, flipped):
    total = None
    for t in range(9):
        start = 160 * (t % 3) + 16 * (t // 3)
        part = padded[field, start : start + 128, 128 * pair : 128 * pair + 256]
        term = multiply(part, band[t], flipped)
        total = term if total is None else total + term
    return total


def filter_taps(t, late, padded, sums):
    low = lax.broadcasted_iota(jnp.int32, (C, 128), 1) < C
    one = None
    two = None
    at_one = pl.multiple_of(160 * (t % 3) + 16 * (t // 3), 16)
    back = 8 - t
    at_two = pl.multiple_of(160 * (back % 3) + 16 * (back // 3), 16)
    for pair in range(4):
        lanes = slice(128 * pair, 128 * pair + 128)
        wide = slice(128 * pair, 128 * pair + 256)
        ghid = late[GHID, 1:9, :, lanes].reshape(128, 128)
        middle = late[MID, 1:9, :, lanes].reshape(128, 128)
        term = lax.dot_general(
            padded[FEAT, pl.ds(at_one, 128), wide], ghid, TN, preferred_element_type=F32
        )
        one = term if one is None else one + term
        term = lax.dot_general(
            middle, padded[GOUT, pl.ds(at_two, 128), wide], TN, preferred_element_type=F32
        )
        two = term if two is None else two + term
    for e in range(3):
        near = one[C * e : C * e + C]
        far = one[C * e + C : C * e + 2 * C]
        pieces = []
        for value, block in ((two[:C], 2 - e), (two[C:], 3 - e)):
            tile = value[:, 128 * (block // 2) : 128 * (block // 2) + 128]
            pieces.append(tile if block % 2 else pltpu.roll(tile, C, 1))
        first_part = near + pltpu.roll(far, C, 1)
        second_part = pieces[0] + pieces[1]
        start = pl.multiple_of(192 * t + C * e, C)
        sums[pl.ds(start, C), :] = jnp.where(low, first_part, second_part)


def halo_copies(places, send, recv, count, me):
    devices = ((me + 1) % count, (me + count - 1) % count)
    return [
        pltpu.make_async_remote_copy(
            src_ref=source,
            dst_ref=target,
            send_sem=send.at[i],
            recv_sem=recv.at[i],
            device_id={"dom": devices[i % 2]},
        )
        for i, (source, target) in enumerate(places)
    ]


def halo_start(copies, count, me):
    @pl.when(me < count - 1)
    def _():
        for copy in copies[::2]:
            copy.start()

    @pl.when(me > 0)
    def _():
        for copy in copies[1::2]:
            copy.start()


def halo_wait(copies, count, me):
    @pl.when(me < count - 1)
    def _():
        for copy in copies[::2]:
            copy.wait_send()
        for copy in copies[1::2]:
            copy.wait_recv()

    @pl.when(me > 0)
    def _():
        for copy in copies[1::2]:
            copy.wait_send()
        for copy in copies[::2]:
            copy.wait_recv()


def prepare(
    count,
    feat_in, wa_in, wb_in, nb_in, act_in, cot_in,
    given, padded, sel, sel_edge, band_a, band_at, band_b, band_bt, alive,
    feat, cot, wa, wb, nb, act, edge,
    in_sem, halo_send, halo_recv,
):
    me = lax.axis_index("dom")
    edge[...] = jnp.zeros(edge.shape, BF16)
    barrier = pltpu.get_barrier_semaphore()
    pl.semaphore_signal(barrier, inc=1, device_id={"dom": (me + 1) % count})
    pl.semaphore_signal(barrier, inc=1, device_id={"dom": (me + count - 1) % count})
    loads = [
        pltpu.make_async_copy(source, target, in_sem.at[i])
        for i, (source, target) in enumerate(
            ((act_in, act), (feat_in, feat), (cot_in, cot), (nb_in, nb), (wa_in, wa), (wb_in, wb))
        )
    ]
    for load in loads:
        load.start()
    pl.semaphore_wait(barrier, 2)
    places = []
    for field, values in ((FEAT, feat_in), (GOUT, cot_in)):
        places.append((values.at[:, E - 1], edge.at[field, 0]))
        places.append((values.at[:, 0], edge.at[field, 1]))
    halo = halo_copies(places, halo_send, halo_recv, count, me)
    halo_start(halo, count, me)
    for load in loads[:4]:
        load.wait()
    keep = [jnp.where(act[b] > 0, 1.0, 0.0) for b in range(2)]
    given[FEAT] = jnp.concatenate([feat[b].astype(F32) for b in range(2)], axis=1).astype(BF16)
    given[GOUT] = jnp.concatenate(
        [cot[b].astype(F32) * keep[b] for b in range(2)], axis=1
    ).astype(BF16)
    rows = lax.broadcasted_iota(jnp.int32, (128, 128), 0)
    alive[...] = jnp.where((rows & 8) == 0, keep[0], keep[1])
    build_selection(nb, sel, sel_edge)
    for field in (FEAT, GOUT):
        pad_inner(given[field], sel, padded, field)
    for load in loads[4:]:
        load.wait()
    build_bands(wa, band_a, band_at)
    build_bands(wb, band_b, band_bt)
    halo_wait(halo, count, me)
    for field in (FEAT, GOUT):
        below, above = [
            edge[field, side].astype(F32).reshape(16, 512).astype(BF16) for side in range(2)
        ]
        pad_edge(below, above, sel_edge, padded, field)


def kernel(
    ny, nz, scale,
    given, padded, sel, sel_edge, band_a, band_at, band_b, band_bt, alive,
    out, gfeat, full,
    late, late_padded, sums, from_core, chip, from_plane, groups,
    halo_send, halo_recv, core_send, core_recv, plane_send, plane_recv,
    group_send, group_recv, back_send, back_recv, last_send, last_recv, relay,
):
    count = ny * nz * NCORE
    plane = ny * ZLOW
    nhigh = nz // ZLOW
    live = -(-HALF // CH)
    me = lax.axis_index("dom")
    core = me % NCORE
    y = me // (NCORE * nz)
    z = (me // NCORE) % nz
    zlow = z % ZLOW
    zhigh = z // ZLOW
    spot = y * ZLOW + zlow
    partner = me + 1 - 2 * core
    steps = [(dy, dz) for dy in range(ny) for dz in range(ZLOW) if dy or dz]
    order = sorted(
        range(len(steps)),
        key=lambda i: (0, 1, 2, 1)[steps[i][0]] + (0, 1, 1, 2)[steps[i][1]],
        reverse=True,
    )

    def ahead(i):
        dy, dz = steps[i]
        return y ^ dy, (z + nz + (0, 1, -1, 2 - 4 * core)[dz]) % nz

    def behind(i):
        dy, dz = steps[i]
        return y ^ dy, (z + nz - (0, 1, -1, 2 - 4 * core)[dz]) % nz

    def device_at(place):
        return (place[0] * nz + place[1]) * NCORE + core

    def spot_at(place):
        return place[0] * ZLOW + place[1] % ZLOW

    def at_group(step):
        return device_at((y, (z + step * ZLOW) % nz))

    near = sorted({1, nhigh - 1})
    far = nhigh > 3
    greeted = [device_at(ahead(i)) for i in order]
    greeted += [device_at(behind(i)) for i in order if steps[i][1] == 3]
    greeted += [at_group(step) for step in (near if far else range(1, nhigh))]
    greeted += [(me + 1) % count, (me + count - 1) % count]
    late[:, 0] = jnp.zeros((2, 16, 512), BF16)
    late[:, 9] = jnp.zeros((2, 16, 512), BF16)
    barrier = pltpu.get_barrier_semaphore()
    for device in greeted:
        pl.semaphore_signal(barrier, inc=1, device_id={"dom": device})

    chip[HALF:, :] = jnp.zeros((CH * plane - HALF, 128), BF16)
    for pair in range(4):
        lanes = slice(128 * pair, 128 * pair + 128)
        h = convolve(padded, FEAT, band_a, pair, False)
        g = convolve(padded, GOUT, band_bt, pair, True)
        s = jax.nn.sigmoid(h)
        middle = alive[...] * (h * s)
        ghid = g * (s * (1.0 + h * (1.0 - s)))
        late[MID, 1:9, :, lanes] = middle.astype(BF16).reshape(8, 16, 128)
        late[GHID, 1:9, :, lanes] = ghid.astype(BF16).reshape(8, 16, 128)
    for i in range(5):
        filter_taps(4 * (1 - core) + i, late, padded, sums)
    pl.semaphore_wait(barrier, len(greeted))
    if far:
        for step in near:
            pl.semaphore_signal(relay, inc=1, device_id={"dom": at_group(step)})

    own = pl.multiple_of(core * HALF, 8)
    other = pl.multiple_of((1 - core) * HALF, 8)
    to_core = pltpu.make_async_remote_copy(
        src_ref=sums.at[pl.ds(other, HALF)],
        dst_ref=from_core,
        send_sem=core_send,
        recv_sem=core_recv,
        device_id={"dom": partner},
    )
    to_core.start()
    halo = halo_copies(
        ((late.at[:, E], late.at[:, 0]), (late.at[:, 1], late.at[:, E + 1])),
        halo_send, halo_recv, count, me,
    )
    halo_start(halo, count, me)
    for i in range(4):
        filter_taps(5 * core + i, late, padded, sums)
    to_core.wait_recv()
    from_core[...] = from_core[...] + sums[pl.ds(own, HALF), :]
    chip[:HALF, :] = from_core[...].astype(BF16)

    def plane_copy(i):
        begin = pl.multiple_of(spot_at(ahead(i)) * CH, CH)
        return pltpu.make_async_remote_copy(
            src_ref=chip.at[pl.ds(begin, CH)],
            dst_ref=from_plane.at[i],
            send_sem=plane_send.at[i],
            recv_sem=plane_recv.at[i],
            device_id={"dom": device_at(ahead(i))},
        )

    for i in order:

        @pl.when(spot_at(ahead(i)) < live)
        def _():
            plane_copy(i).start()

    def last(field, band, flipped, target, base):
        for pair in range(4):
            lanes = slice(128 * pair, 128 * pair + 128)
            value = convolve(late_padded, field, band, pair, flipped)
            if flipped:
                value = value * alive[...]
            value = value.reshape(8, 16, 128) + given[base, :, :, lanes].astype(F32)
            for b in range(2):
                target[b, :, :, lanes] = value[:, 8 * b : 8 * b + 8].astype(BF16)

    halo_wait(halo, count, me)
    for field in (MID, GHID):
        pad_inner(late[field, 1:9], sel, late_padded, field)
        pad_edge(late[field, 0], late[field, 9], sel_edge, late_padded, field)
    last(MID, band_b, False, out, FEAT)

    to_group = [
        pltpu.make_async_remote_copy(
            src_ref=groups.at[zhigh],
            dst_ref=groups.at[zhigh],
            send_sem=group_send.at[step - 1],
            recv_sem=group_recv.at[step - 1],
            device_id={"dom": at_group(step)},
        )
        for step in sorted(range(1, nhigh), key=lambda step: -min(step, nhigh - step))
    ]
    back = [
        pltpu.make_async_remote_copy(
            src_ref=full.at[core, spot],
            dst_ref=full.at[core, spot],
            send_sem=back_send.at[i],
            recv_sem=back_recv.at[i],
            device_id={"dom": device_at(behind(i))},
        )
        for i in range(len(steps))
    ]

    def forward(place):
        return pltpu.make_async_remote_copy(
            src_ref=full.at[core, place],
            dst_ref=full.at[core, place],
            send_sem=last_send.at[place],
            recv_sem=last_recv.at[place],
            device_id={"dom": partner},
        )

    if far:
        pl.semaphore_wait(relay, len(near))

    @pl.when(spot < live)
    def _():
        total = chip[pl.ds(pl.multiple_of(spot * CH, CH), CH), :].astype(F32)
        for i in order:
            plane_copy(i).wait_recv()
        for i in range(len(steps)):
            total = total + from_plane[i].astype(F32)
        groups[zhigh] = total.astype(BF16)
        for copy in to_group:
            copy.start()

    last(GHID, band_at, True, gfeat, GOUT)

    @pl.when(spot < live)
    def _():
        for copy in to_group:
            copy.wait_recv()
        total = groups[0].astype(F32)
        for i in range(1, nhigh):
            total = total + groups[i].astype(F32)
        full[core, spot] = (total * scale).astype(BF16)
        for i in order:
            back[i].start()
        forward(spot).start()

    to_core.wait_send()
    for i in order:

        @pl.when(spot_at(ahead(i)) < live)
        def _():
            plane_copy(i).wait_send()

    for i in order[::-1]:

        @pl.when(spot_at(ahead(i)) < live)
        def _():
            back[i].wait_recv()
            forward(spot_at(ahead(i))).start()

    @pl.when(spot < live)
    def _():
        for copy in to_group:
            copy.wait_send()
        for copy in back:
            copy.wait_send()

    for place in range(live):
        forward(place).wait()


def finish(out_in, gfeat_in, full, out, gfeat, fa, fb, fa_here, fb_here, sems):
    copies = [
        pltpu.make_async_copy(out_in, out, sems.at[0]),
        pltpu.make_async_copy(gfeat_in, gfeat, sems.at[1]),
    ]
    for copy in copies:
        copy.start()
    for h in range(NCORE):
        rows = slice(h * HALF, h * HALF + HALF)
        value = full[h].reshape(full.shape[1] * CH, 128)[:HALF].astype(F32)
        fa_here[rows, :] = value[:, :C]
        fb_here[rows, :] = pltpu.roll(value, C, 1)[:, :C]
        for i, (here, there) in enumerate(((fa_here, fa), (fb_here, fb))):
            copy = pltpu.make_async_copy(here.at[rows], there.at[rows], sems.at[2 + 2 * h + i])
            copy.start()
            copies.append(copy)
    for copy in copies:
        copy.wait()


def on_device(ny, nz, features, weight_first, weight_second, neighbours, active, cotangent):
    count = ny * nz * NCORE
    scale = 1.0 / math.sqrt(2 * count * E**3)
    plane = ny * ZLOW
    nhigh = nz // ZLOW
    vmem = pl.BlockSpec(memory_space=pltpu.VMEM)
    hbm = pl.BlockSpec(memory_space=pltpu.HBM)
    dma = pltpu.SemaphoreType.DMA
    brick = jax.ShapeDtypeStruct(features.shape, BF16)
    whole = pltpu.VMEM(features.shape, BF16)
    taps = pltpu.VMEM(weight_first.shape, BF16)
    prepared = pl.pallas_call(
        functools.partial(prepare, count),
        out_shape=(
            jax.ShapeDtypeStruct((2, 8, 16, 512), BF16),
            jax.ShapeDtypeStruct((2, 480, 640), BF16),
            jax.ShapeDtypeStruct((3, 384, 128), BF16),
            jax.ShapeDtypeStruct((3, 96, 32), BF16),
            jax.ShapeDtypeStruct((9, 256, 128), BF16),
            jax.ShapeDtypeStruct((9, 128, 256), BF16),
            jax.ShapeDtypeStruct((9, 256, 128), BF16),
            jax.ShapeDtypeStruct((9, 128, 256), BF16),
            jax.ShapeDtypeStruct((128, 128), F32),
        ),
        in_specs=[hbm] * 6,
        out_specs=(vmem,) * 9,
        scratch_shapes=[
            whole, whole, taps, taps,
            pltpu.SMEM(neighbours.shape, jnp.int32),
            pltpu.SMEM(active.shape, jnp.int32),
            pltpu.VMEM((2, 2, 2, E, 512), BF16),
            dma((6,)), dma((4,)), dma((4,)),
        ],
        compiler_params=pltpu.CompilerParams(
            collective_id=0, has_side_effects=True, vmem_limit_bytes=24 * 2**20
        ),
    )(
        *[
            pltpu.with_memory_space_constraint(value, pltpu.HBM)
            for value in (
                features, weight_first, weight_second, neighbours, active, cotangent
            )
        ]
    )
    out, gfeat, full = pl.pallas_call(
        functools.partial(kernel, ny, nz, scale),
        out_shape=(brick, brick, jax.ShapeDtypeStruct((NCORE, plane, CH, 128), BF16)),
        in_specs=[vmem] * 9,
        out_specs=(vmem, vmem, vmem),
        scratch_shapes=[
            pltpu.VMEM((2, 10, 16, 512), BF16),
            pltpu.VMEM((2, 480, 640), BF16),
            pltpu.VMEM((ROWS, 128), F32),
            pltpu.VMEM((HALF, 128), F32),
            pltpu.VMEM((plane * CH, 128), BF16),
            pltpu.VMEM((plane - 1, CH, 128), BF16),
            pltpu.VMEM((nhigh, CH, 128), BF16),
            dma((2,)), dma((2,)),
            dma, dma,
            dma((plane - 1,)), dma((plane - 1,)),
            dma((nhigh - 1,)), dma((nhigh - 1,)),
            dma((plane - 1,)), dma((plane - 1,)),
            dma((plane,)), dma((plane,)),
            pltpu.SemaphoreType.REGULAR,
        ],
        compiler_params=pltpu.CompilerParams(
            collective_id=1, has_side_effects=True, vmem_limit_bytes=24 * 2**20
        ),
    )(*prepared)
    grads = jax.ShapeDtypeStruct((ROWS, C), F32)
    out, gfeat, fa, fb = pl.pallas_call(
        finish,
        out_shape=(brick, brick, grads, grads),
        in_specs=[vmem] * 3,
        out_specs=(hbm,) * 4,
        scratch_shapes=[pltpu.VMEM((ROWS, C), F32), pltpu.VMEM((ROWS, C), F32), dma((6,))],
        compiler_params=pltpu.CompilerParams(vmem_limit_bytes=24 * 2**20),
    )(out, gfeat, full)
    return out, gfeat, fa.reshape(3, 3, 3, C, C), fb.reshape(3, 3, 3, C, C)


def solution(mesh):
    count = mesh.shape["dom"]
    return jax.shard_map(
        functools.partial(on_device, count // (NZ * NCORE), NZ),
        mesh=mesh,
        in_specs=(
            P(("scene", "dom"), None, None, None),
            P(),
            P(),
            P(("scene", "dom"), None),
            P(("scene", "dom")),
            P(("scene", "dom"), None, None, None),
        ),
        out_specs=(
            P(("scene", "dom"), None, None, None),
            P(("scene", "dom"), None, None, None),
            P("scene", None, None, None, None),
            P("scene", None, None, None, None),
        ),
        check_vma=False,
    )
```

```python
import functools
import math

import jax
import jax.numpy as jnp
from jax import lax
from jax.experimental import pallas as pl
from jax.experimental.pallas import tpu as pltpu
from jax.sharding import PartitionSpec as P

C = 64
E = 8
FEAT, GOUT = 0, 1
MID, GHID = 0, 1
TN = (((0,), (0,)), ((), ()))
NT = (((1,), (1,)), ((), ()))
ROWS = 27 * C
HALF = ROWS // 2
NCORE = 2
NZ = 16
ZLOW = 4
CH = 64
F32 = jnp.float32
BF16 = jnp.bfloat16


def entry(nb, brick, offset):
    if offset == (0, 0, 0):
        return 8 * brick
    place = (offset[0] + 1) * 9 + (offset[1] + 1) * 3 + offset[2] + 1
    ident = nb[brick, place if place < 13 else place - 1]
    return jnp.where(ident < 0, -1000, (ident & 1) * 8)


def build_selection(nb, sel, sel_edge):
    row = lax.broadcasted_iota(jnp.int32, (16, 128), 0)
    lane = lax.broadcasted_iota(jnp.int32, (16, 128), 1)
    y = row & 7
    second = row >= 8
    for iz in range(3):
        for c in range(3):
            yy = y + (c - 1)
            wrap = (yy < 0) | (yy > 7)
            for ix in range(3):
                codes = []
                for brick in range(2):
                    inner = entry(nb, brick, (ix - 1, 0, iz - 1))
                    if c == 1:
                        codes.append(jnp.full((16, 128), inner, jnp.int32))
                    else:
                        outer = entry(nb, brick, (ix - 1, c - 1, iz - 1))
                        codes.append(jnp.where(wrap, outer, inner))
                target = jnp.where(second, codes[1], codes[0]) + (yy & 7)
                if ix == 1:
                    for x in range(8):
                        hit = jnp.where(lane == target + 16 * x, 1.0, 0.0).astype(BF16)
                        sel[iz, 128 * c + 16 * x : 128 * c + 16 * x + 16, :] = hit
                else:
                    side = ix // 2
                    hit = jnp.where(lane == target + 16 * side, 1.0, 0.0).astype(BF16)
                    sel_edge[iz, 32 * c + 16 * side : 32 * c + 16 * side + 16, :] = hit[:, :32]


def build_bands(weight, band, band_t):
    zero = jnp.zeros((C, C), BF16)
    for t in range(9):
        taps = [weight[t // 3, t % 3, e] for e in range(3)]
        for zi in range(4):
            left = taps[zi] if zi < 3 else zero
            right = taps[zi - 1] if zi > 0 else zero
            band[t, C * zi : C * zi + C, :] = jnp.concatenate([left, right], axis=1)
        band_t[8 - t, :C, :] = jnp.concatenate([taps[2], taps[1], taps[0], zero], axis=1)
        band_t[8 - t, C:, :] = jnp.concatenate([zero, taps[2], taps[1], taps[0]], axis=1)


def select(source, choose):
    rows = choose.shape[1]
    low = lax.broadcasted_iota(jnp.int32, (rows, 128), 1) < C
    source = pltpu.roll(source.astype(F32), C, 1).astype(BF16)
    edge = source[:, :128]
    inner = jnp.dot(choose[1], source, preferred_element_type=F32)
    before = jnp.dot(choose[0], edge, preferred_element_type=F32)
    after = jnp.dot(choose[2], edge, preferred_element_type=F32)
    first = jnp.where(low, before, inner[:, :128])
    last = jnp.where(low, inner[:, :128], after)
    return jnp.concatenate([first, inner[:, 128:], last], axis=1).astype(BF16)


def pad_inner(layers, sel, padded, field):
    value = select(layers.reshape(128, 512), sel)
    for c in range(3):
        start = 160 * c + 16
        padded[field, start : start + 128, :] = value[128 * c : 128 * c + 128]


def pad_edge(below, above, sel_edge, padded, field):
    value = select(jnp.concatenate([below, above], axis=0), sel_edge)
    for c in range(3):
        padded[field, 160 * c : 160 * c + 16, :] = value[32 * c : 32 * c + 16]
        padded[field, 160 * c + 144 : 160 * c + 160, :] = value[32 * c + 16 : 32 * c + 32]


def multiply(part, tap, flipped):
    if flipped:
        return lax.dot_general(part, tap, NT, preferred_element_type=F32)
    return jnp.dot(part, tap, preferred_element_type=F32)


def convolve(padded, field, band, pair, flipped):
    total = None
    for t in range(9):
        start = 160 * (t % 3) + 16 * (t // 3)
        part = padded[field, start : start + 128, 128 * pair : 128 * pair + 256]
        term = multiply(part, band[t], flipped)
        total = term if total is None else total + term
    return total


def convolve_edge(padded, field, band, flipped):
    sides = []
    for layer, a in ((0, 0), (9, 2)):
        total = None
        for c in range(3):
            start = 160 * c + 16 * layer
            part = jnp.concatenate(
                [
                    padded[field, start : start + 16, 128 * pair : 128 * pair + 256]
                    for pair in range(4)
                ],
                axis=0,
            )
            term = multiply(part, band[3 * a + c], flipped)
            total = term if total is None else total + term
        sides.append(total)
    return sides


def filter_taps(t, late, padded, sums):
    low = lax.broadcasted_iota(jnp.int32, (C, 128), 1) < C
    one = None
    two = None
    at_one = pl.multiple_of(160 * (t % 3) + 16 * (t // 3), 16)
    back = 8 - t
    at_two = pl.multiple_of(160 * (back % 3) + 16 * (back // 3), 16)
    for pair in range(4):
        lanes = slice(128 * pair, 128 * pair + 128)
        wide = slice(128 * pair, 128 * pair + 256)
        ghid = late[GHID, 1:9, :, lanes].reshape(128, 128)
        middle = late[MID, 1:9, :, lanes].reshape(128, 128)
        term = lax.dot_general(
            padded[FEAT, pl.ds(at_one, 128), wide], ghid, TN, preferred_element_type=F32
        )
        one = term if one is None else one + term
        term = lax.dot_general(
            middle, padded[GOUT, pl.ds(at_two, 128), wide], TN, preferred_element_type=F32
        )
        two = term if two is None else two + term
    for e in range(3):
        near = one[C * e : C * e + C]
        far = one[C * e + C : C * e + 2 * C]
        pieces = []
        for value, block in ((two[:C], 2 - e), (two[C:], 3 - e)):
            tile = value[:, 128 * (block // 2) : 128 * (block // 2) + 128]
            pieces.append(tile if block % 2 else pltpu.roll(tile, C, 1))
        first_part = near + pltpu.roll(far, C, 1)
        second_part = pieces[0] + pieces[1]
        start = pl.multiple_of(192 * t + C * e, C)
        sums[pl.ds(start, C), :] = jnp.where(low, first_part, second_part)


def halo_copies(places, send, recv, count, me):
    devices = ((me + 1) % count, (me + count - 1) % count)
    return [
        pltpu.make_async_remote_copy(
            src_ref=source,
            dst_ref=target,
            send_sem=send.at[i],
            recv_sem=recv.at[i],
            device_id={"dom": devices[i % 2]},
        )
        for i, (source, target) in enumerate(places)
    ]


def halo_start(copies, count, me):
    @pl.when(me < count - 1)
    def _():
        for copy in copies[::2]:
            copy.start()

    @pl.when(me > 0)
    def _():
        for copy in copies[1::2]:
            copy.start()


def halo_wait(copies, count, me):
    @pl.when(me < count - 1)
    def _():
        for copy in copies[::2]:
            copy.wait_send()
        for copy in copies[1::2]:
            copy.wait_recv()

    @pl.when(me > 0)
    def _():
        for copy in copies[1::2]:
            copy.wait_send()
        for copy in copies[::2]:
            copy.wait_recv()


def kernel(
    ny, nz, scale,
    feat_in, wa_in, wb_in, nb_in, act_in, cot_in,
    out, gfeat, full,
    feat, cot, wa, wb, nb, act, edge, given,
    sel, sel_edge, padded, band_a, band_at, band_b, band_bt,
    late, late_padded, sums, from_core, chip, from_plane, groups,
    in_sem, first_send, first_recv,
    halo_send, halo_recv, core_send, core_recv, plane_send, plane_recv,
    group_send, group_recv, back_send, back_recv, last_send, last_recv, relay,
):
    count = ny * nz * NCORE
    plane = ny * ZLOW
    nhigh = nz // ZLOW
    live = -(-HALF // CH)
    me = lax.axis_index("dom")
    core = me % NCORE
    y = me // (NCORE * nz)
    z = (me // NCORE) % nz
    zlow = z % ZLOW
    zhigh = z // ZLOW
    spot = y * ZLOW + zlow
    partner = me + 1 - 2 * core
    steps = [(dy, dz) for dy in range(ny) for dz in range(ZLOW) if dy or dz]
    order = sorted(
        range(len(steps)),
        key=lambda i: (0, 1, 2, 1)[steps[i][0]] + (0, 1, 1, 2)[steps[i][1]],
        reverse=True,
    )

    def ahead(i):
        dy, dz = steps[i]
        return y ^ dy, (z + nz + (0, 1, -1, 2 - 4 * core)[dz]) % nz

    def behind(i):
        dy, dz = steps[i]
        return y ^ dy, (z + nz - (0, 1, -1, 2 - 4 * core)[dz]) % nz

    def device_at(place):
        return (place[0] * nz + place[1]) * NCORE + core

    def spot_at(place):
        return place[0] * ZLOW + place[1] % ZLOW

    def at_group(step):
        return device_at((y, (z + step * ZLOW) % nz))

    def at_row(step):
        return device_at((y, (z + nz + step) % nz))

    def at_column(step):
        return device_at((y ^ step, z))

    def tell(number, devices):
        for device in devices:
            pl.semaphore_signal(relay.at[number], inc=1, device_id={"dom": device})

    def hear(number, devices):
        if devices:
            pl.semaphore_wait(relay.at[number], len(devices))

    columns = [at_column(step) for step in range(1, ny)]
    ones, twos, fours = [[at_row(step), at_row(-step)] for step in (1, 2, 4)]
    greeted = [(me + 1) % count, (me + count - 1) % count] + ones + columns

    edge[...] = jnp.zeros(edge.shape, BF16)
    late[:, 0] = jnp.zeros((2, 16, 512), BF16)
    late[:, 9] = jnp.zeros((2, 16, 512), BF16)
    barrier = pltpu.get_barrier_semaphore()
    for device in greeted:
        pl.semaphore_signal(barrier, inc=1, device_id={"dom": device})
    loads = [
        pltpu.make_async_copy(source, target, in_sem.at[i])
        for i, (source, target) in enumerate(
            ((act_in, act), (feat_in, feat), (cot_in, cot), (nb_in, nb), (wa_in, wa), (wb_in, wb))
        )
    ]
    for load in loads:
        load.start()
    pl.semaphore_wait(barrier, len(greeted))
    places = []
    for field, values in ((FEAT, feat_in), (GOUT, cot_in)):
        places.append((values.at[:, E - 1], edge.at[field, 0]))
        places.append((values.at[:, 0], edge.at[field, 1]))
    first = halo_copies(places, first_send, first_recv, count, me)
    halo_start(first, count, me)
    tell(0, ones)
    for load in loads[:4]:
        load.wait()
    keep = [jnp.where(act[b] > 0, 1.0, 0.0) for b in range(2)]
    given[FEAT] = jnp.concatenate([feat[b].astype(F32) for b in range(2)], axis=1).astype(BF16)
    given[GOUT] = jnp.concatenate(
        [cot[b].astype(F32) * keep[b] for b in range(2)], axis=1
    ).astype(BF16)
    rows = lax.broadcasted_iota(jnp.int32, (128, 128), 0)
    alive = jnp.where((rows & 8) == 0, keep[0], keep[1])
    build_selection(nb, sel, sel_edge)
    for field in (FEAT, GOUT):
        for c in range(3):
            padded[field, 160 * c : 160 * c + 16, :] = jnp.zeros((16, 640), BF16)
            padded[field, 160 * c + 144 : 160 * c + 160, :] = jnp.zeros((16, 640), BF16)
        pad_inner(given[field], sel, padded, field)
    for load in loads[4:]:
        load.wait()
    build_bands(wa, band_a, band_at)
    build_bands(wb, band_b, band_bt)
    hear(0, ones)
    tell(1, twos)
    tell(2, columns)
    hidden = [convolve(padded, FEAT, band_a, pair, False) for pair in range(4)]
    grad = [convolve(padded, GOUT, band_bt, pair, True) for pair in range(4)]
    halo_wait(first, count, me)
    for field in (FEAT, GOUT):
        below, above = [
            edge[field, side].astype(F32).reshape(16, 512).astype(BF16) for side in range(2)
        ]
        pad_edge(below, above, sel_edge, padded, field)
    hidden_edge = convolve_edge(padded, FEAT, band_a, False)
    grad_edge = convolve_edge(padded, GOUT, band_bt, True)
    for pair in range(4):
        lanes = slice(128 * pair, 128 * pair + 128)
        some = slice(16 * pair, 16 * pair + 16)

        def joined(value, sides):
            return jnp.concatenate(
                [value[:16] + sides[0][some], value[16:112], value[112:] + sides[1][some]], axis=0
            )

        h = joined(hidden[pair], hidden_edge)
        g = joined(grad[pair], grad_edge)
        s = jax.nn.sigmoid(h)
        middle = alive * (h * s)
        ghid = g * (s * (1.0 + h * (1.0 - s)))
        late[MID, 1:9, :, lanes] = middle.astype(BF16).reshape(8, 16, 128)
        late[GHID, 1:9, :, lanes] = ghid.astype(BF16).reshape(8, 16, 128)
    halo = halo_copies(
        ((late.at[:, E], late.at[:, 0]), (late.at[:, 1], late.at[:, E + 1])),
        halo_send, halo_recv, count, me,
    )
    halo_start(halo, count, me)
    hear(1, twos)
    tell(3, fours)
    chip[HALF:, :] = jnp.zeros((CH * plane - HALF, 128), BF16)
    for i in range(5):
        filter_taps(4 * (1 - core) + i, late, padded, sums)

    own = pl.multiple_of(core * HALF, 8)
    other = pl.multiple_of((1 - core) * HALF, 8)
    to_core = pltpu.make_async_remote_copy(
        src_ref=sums.at[pl.ds(other, HALF)],
        dst_ref=from_core,
        send_sem=core_send,
        recv_sem=core_recv,
        device_id={"dom": partner},
    )
    to_core.start()
    for i in range(4):
        filter_taps(5 * core + i, late, padded, sums)
    to_core.wait_recv()
    from_core[...] = from_core[...] + sums[pl.ds(own, HALF), :]
    chip[:HALF, :] = from_core[...].astype(BF16)

    def plane_copy(i):
        begin = pl.multiple_of(spot_at(ahead(i)) * CH, CH)
        return pltpu.make_async_remote_copy(
            src_ref=chip.at[pl.ds(begin, CH)],
            dst_ref=from_plane.at[i],
            send_sem=plane_send.at[i],
            recv_sem=plane_recv.at[i],
            device_id={"dom": device_at(ahead(i))},
        )

    hear(2, columns)
    for i in order:

        @pl.when(spot_at(ahead(i)) < live)
        def _():
            plane_copy(i).start()

    def last(field, band, flipped, target, base):
        for pair in range(4):
            lanes = slice(128 * pair, 128 * pair + 128)
            value = convolve(late_padded, field, band, pair, flipped)
            if flipped:
                value = value * alive
            value = value.reshape(8, 16, 128) + given[base, :, :, lanes].astype(F32)
            for b in range(2):
                target[b, :, :, lanes] = value[:, 8 * b : 8 * b + 8].astype(BF16)

    halo_wait(halo, count, me)
    for field in (MID, GHID):
        pad_inner(late[field, 1:9], sel, late_padded, field)
        pad_edge(late[field, 0], late[field, 9], sel_edge, late_padded, field)
    last(MID, band_b, False, out, FEAT)

    to_group = [
        pltpu.make_async_remote_copy(
            src_ref=groups.at[zhigh],
            dst_ref=groups.at[zhigh],
            send_sem=group_send.at[step - 1],
            recv_sem=group_recv.at[step - 1],
            device_id={"dom": at_group(step)},
        )
        for step in sorted(range(1, nhigh), key=lambda step: -min(step, nhigh - step))
    ]
    back = [
        pltpu.make_async_remote_copy(
            src_ref=full.at[core, spot],
            dst_ref=full.at[core, spot],
            send_sem=back_send.at[i],
            recv_sem=back_recv.at[i],
            device_id={"dom": device_at(behind(i))},
        )
        for i in range(len(steps))
    ]

    def forward(place):
        return pltpu.make_async_remote_copy(
            src_ref=full.at[core, place],
            dst_ref=full.at[core, place],
            send_sem=last_send.at[place],
            recv_sem=last_recv.at[place],
            device_id={"dom": partner},
        )

    hear(3, fours)

    @pl.when(spot < live)
    def _():
        total = chip[pl.ds(pl.multiple_of(spot * CH, CH), CH), :].astype(F32)
        for i in order:
            plane_copy(i).wait_recv()
        for i in range(len(steps)):
            total = total + from_plane[i].astype(F32)
        groups[zhigh] = total.astype(BF16)
        for copy in to_group:
            copy.start()

    last(GHID, band_at, True, gfeat, GOUT)

    @pl.when(spot < live)
    def _():
        for copy in to_group:
            copy.wait_recv()
        total = groups[0].astype(F32)
        for i in range(1, nhigh):
            total = total + groups[i].astype(F32)
        full[core, spot] = (total * scale).astype(BF16)
        for i in order:
            back[i].start()
        forward(spot).start()

    to_core.wait_send()
    for i in order:

        @pl.when(spot_at(ahead(i)) < live)
        def _():
            plane_copy(i).wait_send()

    for i in order[::-1]:

        @pl.when(spot_at(ahead(i)) < live)
        def _():
            back[i].wait_recv()
            forward(spot_at(ahead(i))).start()

    @pl.when(spot < live)
    def _():
        for copy in to_group:
            copy.wait_send()
        for copy in back:
            copy.wait_send()

    for place in range(live):
        forward(place).wait()


def finish(out_in, gfeat_in, full, out, gfeat, fa, fb, fa_here, fb_here, sems):
    copies = [
        pltpu.make_async_copy(out_in, out, sems.at[0]),
        pltpu.make_async_copy(gfeat_in, gfeat, sems.at[1]),
    ]
    for copy in copies:
        copy.start()
    for h in range(NCORE):
        rows = slice(h * HALF, h * HALF + HALF)
        value = full[h].reshape(full.shape[1] * CH, 128)[:HALF].astype(F32)
        fa_here[rows, :] = value[:, :C]
        fb_here[rows, :] = pltpu.roll(value, C, 1)[:, :C]
        for i, (here, there) in enumerate(((fa_here, fa), (fb_here, fb))):
            copy = pltpu.make_async_copy(here.at[rows], there.at[rows], sems.at[2 + 2 * h + i])
            copy.start()
            copies.append(copy)
    for copy in copies:
        copy.wait()


def on_device(ny, nz, features, weight_first, weight_second, neighbours, active, cotangent):
    count = ny * nz * NCORE
    scale = 1.0 / math.sqrt(2 * count * E**3)
    plane = ny * ZLOW
    nhigh = nz // ZLOW
    vmem = pl.BlockSpec(memory_space=pltpu.VMEM)
    hbm = pl.BlockSpec(memory_space=pltpu.HBM)
    dma = pltpu.SemaphoreType.DMA
    brick = jax.ShapeDtypeStruct(features.shape, BF16)
    whole = pltpu.VMEM(features.shape, BF16)
    taps = pltpu.VMEM(weight_first.shape, BF16)
    out, gfeat, full = pl.pallas_call(
        functools.partial(kernel, ny, nz, scale),
        out_shape=(brick, brick, jax.ShapeDtypeStruct((NCORE, plane, CH, 128), BF16)),
        in_specs=[hbm] * 6,
        out_specs=(vmem, vmem, vmem),
        scratch_shapes=[
            whole, whole, taps, taps,
            pltpu.SMEM(neighbours.shape, jnp.int32),
            pltpu.SMEM(active.shape, jnp.int32),
            pltpu.VMEM((2, 2, 2, E, 512), BF16),
            pltpu.VMEM((2, 8, 16, 512), BF16),
            pltpu.VMEM((3, 384, 128), BF16),
            pltpu.VMEM((3, 96, 32), BF16),
            pltpu.VMEM((2, 480, 640), BF16),
            pltpu.VMEM((9, 256, 128), BF16),
            pltpu.VMEM((9, 128, 256), BF16),
            pltpu.VMEM((9, 256, 128), BF16),
            pltpu.VMEM((9, 128, 256), BF16),
            pltpu.VMEM((2, 10, 16, 512), BF16),
            pltpu.VMEM((2, 480, 640), BF16),
            pltpu.VMEM((ROWS, 128), F32),
            pltpu.VMEM((HALF, 128), F32),
            pltpu.VMEM((plane * CH, 128), BF16),
            pltpu.VMEM((plane - 1, CH, 128), BF16),
            pltpu.VMEM((nhigh, CH, 128), BF16),
            dma((6,)), dma((4,)), dma((4,)),
            dma((2,)), dma((2,)),
            dma, dma,
            dma((plane - 1,)), dma((plane - 1,)),
            dma((nhigh - 1,)), dma((nhigh - 1,)),
            dma((plane - 1,)), dma((plane - 1,)),
            dma((plane,)), dma((plane,)),
            pltpu.SemaphoreType.REGULAR((4,)),
        ],
        compiler_params=pltpu.CompilerParams(
            collective_id=0, has_side_effects=True, vmem_limit_bytes=40 * 2**20
        ),
    )(
        *[
            pltpu.with_memory_space_constraint(value, pltpu.HBM)
            for value in (
                features, weight_first, weight_second, neighbours, active, cotangent
            )
        ]
    )
    grads = jax.ShapeDtypeStruct((ROWS, C), F32)
    out, gfeat, fa, fb = pl.pallas_call(
        finish,
        out_shape=(brick, brick, grads, grads),
        in_specs=[vmem] * 3,
        out_specs=(hbm,) * 4,
        scratch_shapes=[pltpu.VMEM((ROWS, C), F32), pltpu.VMEM((ROWS, C), F32), dma((6,))],
        compiler_params=pltpu.CompilerParams(vmem_limit_bytes=24 * 2**20),
    )(out, gfeat, full)
    return out, gfeat, fa.reshape(3, 3, 3, C, C), fb.reshape(3, 3, 3, C, C)


def solution(mesh):
    count = mesh.shape["dom"]
    return jax.shard_map(
        functools.partial(on_device, count // (NZ * NCORE), NZ),
        mesh=mesh,
        in_specs=(
            P(("scene", "dom"), None, None, None),
            P(),
            P(),
            P(("scene", "dom"), None),
            P(("scene", "dom")),
            P(("scene", "dom"), None, None, None),
        ),
        out_specs=(
            P(("scene", "dom"), None, None, None),
            P(("scene", "dom"), None, None, None),
            P("scene", None, None, None, None),
            P("scene", None, None, None, None),
        ),
        check_vma=False,
    )
```

```python
import functools
import math

import jax
import jax.numpy as jnp
from jax import lax
from jax.experimental import pallas as pl
from jax.experimental.pallas import tpu as pltpu
from jax.sharding import PartitionSpec as P

C = 64
E = 8
FEAT, GOUT = 0, 1
MID, GHID = 0, 1
TN = (((0,), (0,)), ((), ()))
NT = (((1,), (1,)), ((), ()))
ROWS = 27 * C
HALF = ROWS // 2
NCORE = 2
NZ = 16
ZLOW = 4
CH = 64
F32 = jnp.float32
BF16 = jnp.bfloat16


def entry(nb, brick, offset):
    if offset == (0, 0, 0):
        return 8 * brick
    place = (offset[0] + 1) * 9 + (offset[1] + 1) * 3 + offset[2] + 1
    ident = nb[brick, place if place < 13 else place - 1]
    return jnp.where(ident < 0, -1000, (ident & 1) * 8)


def build_selection(nb, sel, sel_edge):
    row = lax.broadcasted_iota(jnp.int32, (16, 128), 0)
    lane = lax.broadcasted_iota(jnp.int32, (16, 128), 1)
    y = row & 7
    second = row >= 8
    for iz in range(3):
        for c in range(3):
            yy = y + (c - 1)
            wrap = (yy < 0) | (yy > 7)
            for ix in range(3):
                codes = []
                for brick in range(2):
                    inner = entry(nb, brick, (ix - 1, 0, iz - 1))
                    if c == 1:
                        codes.append(jnp.full((16, 128), inner, jnp.int32))
                    else:
                        outer = entry(nb, brick, (ix - 1, c - 1, iz - 1))
                        codes.append(jnp.where(wrap, outer, inner))
                target = jnp.where(second, codes[1], codes[0]) + (yy & 7)
                if ix == 1:
                    for x in range(8):
                        hit = jnp.where(lane == target + 16 * x, 1.0, 0.0).astype(BF16)
                        sel[iz, 128 * c + 16 * x : 128 * c + 16 * x + 16, :] = hit
                else:
                    side = ix // 2
                    hit = jnp.where(lane == target + 16 * side, 1.0, 0.0).astype(BF16)
                    sel_edge[iz, 32 * c + 16 * side : 32 * c + 16 * side + 16, :] = hit[:, :32]


def build_band(weight, band):
    zero = jnp.zeros((C, C), BF16)
    for t in range(9):
        taps = [weight[t // 3, t % 3, e] for e in range(3)]
        for zi in range(4):
            left = taps[zi] if zi < 3 else zero
            right = taps[zi - 1] if zi > 0 else zero
            band[t, C * zi : C * zi + C, :] = jnp.concatenate([left, right], axis=1)


def build_flipped(weight, band_t):
    zero = jnp.zeros((C, C), BF16)
    for t in range(9):
        taps = [weight[t // 3, t % 3, e] for e in range(3)]
        band_t[8 - t, :C, :] = jnp.concatenate([taps[2], taps[1], taps[0], zero], axis=1)
        band_t[8 - t, C:, :] = jnp.concatenate([zero, taps[2], taps[1], taps[0]], axis=1)


def select(source, choose):
    rows = choose.shape[1]
    low = lax.broadcasted_iota(jnp.int32, (rows, 128), 1) < C
    source = pltpu.roll(source.astype(F32), C, 1).astype(BF16)
    edge = source[:, :128]
    inner = jnp.dot(choose[1], source, preferred_element_type=F32)
    before = jnp.dot(choose[0], edge, preferred_element_type=F32)
    after = jnp.dot(choose[2], edge, preferred_element_type=F32)
    first = jnp.where(low, before, inner[:, :128])
    last = jnp.where(low, inner[:, :128], after)
    return jnp.concatenate([first, inner[:, 128:], last], axis=1).astype(BF16)


def pad_inner(layers, sel, padded, field):
    value = select(layers.reshape(128, 512), sel)
    for c in range(3):
        start = 160 * c + 16
        padded[field, start : start + 128, :] = value[128 * c : 128 * c + 128]


def pad_edge(below, above, sel_edge, padded, field):
    value = select(jnp.concatenate([below, above], axis=0), sel_edge)
    for c in range(3):
        padded[field, 160 * c : 160 * c + 16, :] = value[32 * c : 32 * c + 16]
        padded[field, 160 * c + 144 : 160 * c + 160, :] = value[32 * c + 16 : 32 * c + 32]


def multiply(part, tap, flipped):
    if flipped:
        return lax.dot_general(part, tap, NT, preferred_element_type=F32)
    return jnp.dot(part, tap, preferred_element_type=F32)


def convolve(padded, field, band, pair, flipped):
    total = None
    for t in range(9):
        start = 160 * (t % 3) + 16 * (t // 3)
        part = padded[field, start : start + 128, 128 * pair : 128 * pair + 256]
        term = multiply(part, band[t], flipped)
        total = term if total is None else total + term
    return total


def convolve_edge(padded, field, band, flipped):
    sides = []
    for layer, a in ((0, 0), (9, 2)):
        total = None
        for c in range(3):
            start = 160 * c + 16 * layer
            part = jnp.concatenate(
                [
                    padded[field, start : start + 16, 128 * pair : 128 * pair + 256]
                    for pair in range(4)
                ],
                axis=0,
            )
            term = multiply(part, band[3 * a + c], flipped)
            total = term if total is None else total + term
        sides.append(total)
    return sides


def filter_taps(t, late, padded, sums):
    low = lax.broadcasted_iota(jnp.int32, (C, 128), 1) < C
    one = None
    two = None
    at_one = pl.multiple_of(160 * (t % 3) + 16 * (t // 3), 16)
    back = 8 - t
    at_two = pl.multiple_of(160 * (back % 3) + 16 * (back // 3), 16)
    for pair in range(4):
        lanes = slice(128 * pair, 128 * pair + 128)
        wide = slice(128 * pair, 128 * pair + 256)
        ghid = late[GHID, 1:9, :, lanes].reshape(128, 128)
        middle = late[MID, 1:9, :, lanes].reshape(128, 128)
        term = lax.dot_general(
            padded[FEAT, pl.ds(at_one, 128), wide], ghid, TN, preferred_element_type=F32
        )
        one = term if one is None else one + term
        term = lax.dot_general(
            middle, padded[GOUT, pl.ds(at_two, 128), wide], TN, preferred_element_type=F32
        )
        two = term if two is None else two + term
    for e in range(3):
        near = one[C * e : C * e + C]
        far = one[C * e + C : C * e + 2 * C]
        pieces = []
        for value, block in ((two[:C], 2 - e), (two[C:], 3 - e)):
            tile = value[:, 128 * (block // 2) : 128 * (block // 2) + 128]
            pieces.append(tile if block % 2 else pltpu.roll(tile, C, 1))
        first_part = near + pltpu.roll(far, C, 1)
        second_part = pieces[0] + pieces[1]
        start = pl.multiple_of(192 * t + C * e, C)
        sums[pl.ds(start, C), :] = jnp.where(low, first_part, second_part)


def halo_copies(places, send, recv, count, me):
    devices = ((me + 1) % count, (me + count - 1) % count)
    return [
        pltpu.make_async_remote_copy(
            src_ref=source,
            dst_ref=target,
            send_sem=send.at[i],
            recv_sem=recv.at[i],
            device_id={"dom": devices[i % 2]},
        )
        for i, (source, target) in enumerate(places)
    ]


def halo_start(copies, count, me):
    @pl.when(me < count - 1)
    def _():
        for copy in copies[::2]:
            copy.start()

    @pl.when(me > 0)
    def _():
        for copy in copies[1::2]:
            copy.start()


def halo_wait(copies, count, me):
    @pl.when(me < count - 1)
    def _():
        for copy in copies[::2]:
            copy.wait_send()
        for copy in copies[1::2]:
            copy.wait_recv()

    @pl.when(me > 0)
    def _():
        for copy in copies[1::2]:
            copy.wait_send()
        for copy in copies[::2]:
            copy.wait_recv()


def kernel(
    ny, nz, scale,
    feat_in, wa_in, wb_in, nb_in, act_in, cot_in,
    out, gfeat, full,
    feat, cot, wa, wb, nb, act, edge, given,
    sel, sel_edge, padded, band_a, band_at, band_b, band_bt,
    late, late_padded, sums, from_core, chip, from_plane, groups,
    in_sem, first_send, first_recv,
    halo_send, halo_recv, core_send, core_recv, plane_send, plane_recv,
    group_send, group_recv, back_send, back_recv, last_send, last_recv, relay,
):
    count = ny * nz * NCORE
    plane = ny * ZLOW
    nhigh = nz // ZLOW
    live = -(-HALF // CH)
    me = lax.axis_index("dom")
    core = me % NCORE
    y = me // (NCORE * nz)
    z = (me // NCORE) % nz
    zlow = z % ZLOW
    zhigh = z // ZLOW
    spot = y * ZLOW + zlow
    partner = me + 1 - 2 * core
    steps = [(dy, dz) for dy in range(ny) for dz in range(ZLOW) if dy or dz]
    order = sorted(
        range(len(steps)),
        key=lambda i: (0, 1, 2, 1)[steps[i][0]] + (0, 1, 1, 2)[steps[i][1]],
        reverse=True,
    )

    def ahead(i):
        dy, dz = steps[i]
        return y ^ dy, (z + nz + (0, 1, -1, 2 - 4 * core)[dz]) % nz

    def behind(i):
        dy, dz = steps[i]
        return y ^ dy, (z + nz - (0, 1, -1, 2 - 4 * core)[dz]) % nz

    def device_at(place):
        return (place[0] * nz + place[1]) * NCORE + core

    def spot_at(place):
        return place[0] * ZLOW + place[1] % ZLOW

    def at_group(step):
        return device_at((y, (z + step * ZLOW) % nz))

    def at_row(step):
        return device_at((y, (z + nz + step) % nz))

    def at_column(step):
        return device_at((y ^ step, z))

    def tell(number, devices):
        for device in devices:
            pl.semaphore_signal(relay.at[number], inc=1, device_id={"dom": device})

    def hear(number, devices):
        if devices:
            pl.semaphore_wait(relay.at[number], len(devices))

    columns = [at_column(step) for step in range(1, ny)]
    ones, twos, fours = [[at_row(step), at_row(-step)] for step in (1, 2, 4)]
    greeted = [(me + 1) % count, (me + count - 1) % count] + ones + columns

    edge[...] = jnp.zeros(edge.shape, BF16)
    late[:, 0] = jnp.zeros((2, 16, 512), BF16)
    late[:, 9] = jnp.zeros((2, 16, 512), BF16)
    barrier = pltpu.get_barrier_semaphore()
    for device in greeted:
        pl.semaphore_signal(barrier, inc=1, device_id={"dom": device})
    loads = [
        pltpu.make_async_copy(source, target, in_sem.at[i])
        for i, (source, target) in enumerate(
            ((act_in, act), (feat_in, feat), (cot_in, cot), (nb_in, nb), (wa_in, wa), (wb_in, wb))
        )
    ]
    for load in loads:
        load.start()
    for load in loads[:4]:
        load.wait()
    keep = [jnp.where(act[b] > 0, 1.0, 0.0) for b in range(2)]
    given[FEAT] = jnp.concatenate([feat[b].astype(F32) for b in range(2)], axis=1).astype(BF16)
    given[GOUT] = jnp.concatenate(
        [cot[b].astype(F32) * keep[b] for b in range(2)], axis=1
    ).astype(BF16)
    rows = lax.broadcasted_iota(jnp.int32, (128, 128), 0)
    alive = jnp.where((rows & 8) == 0, keep[0], keep[1])
    build_selection(nb, sel, sel_edge)
    pl.semaphore_wait(barrier, len(greeted))
    places = []
    for field, values in ((FEAT, feat_in), (GOUT, cot_in)):
        places.append((values.at[:, E - 1], edge.at[field, 0]))
        places.append((values.at[:, 0], edge.at[field, 1]))
    first = halo_copies(places, first_send, first_recv, count, me)
    halo_start(first, count, me)
    tell(0, ones)
    for field in (FEAT, GOUT):
        for c in range(3):
            padded[field, 160 * c : 160 * c + 16, :] = jnp.zeros((16, 640), BF16)
            padded[field, 160 * c + 144 : 160 * c + 160, :] = jnp.zeros((16, 640), BF16)
        pad_inner(given[field], sel, padded, field)
    for load in loads[4:]:
        load.wait()
    build_band(wa, band_a)
    build_flipped(wb, band_bt)
    hear(0, ones)
    tell(1, twos)
    tell(2, columns)
    hidden = [convolve(padded, FEAT, band_a, pair, False) for pair in range(4)]
    grad = [convolve(padded, GOUT, band_bt, pair, True) for pair in range(4)]
    halo_wait(first, count, me)
    for field in (FEAT, GOUT):
        below, above = [
            edge[field, side].astype(F32).reshape(16, 512).astype(BF16) for side in range(2)
        ]
        pad_edge(below, above, sel_edge, padded, field)
    hidden_edge = convolve_edge(padded, FEAT, band_a, False)
    grad_edge = convolve_edge(padded, GOUT, band_bt, True)
    for pair in range(4):
        lanes = slice(128 * pair, 128 * pair + 128)
        some = slice(16 * pair, 16 * pair + 16)

        def joined(value, sides):
            return jnp.concatenate(
                [value[:16] + sides[0][some], value[16:112], value[112:] + sides[1][some]], axis=0
            )

        h = joined(hidden[pair], hidden_edge)
        g = joined(grad[pair], grad_edge)
        s = jax.nn.sigmoid(h)
        middle = alive * (h * s)
        ghid = g * (s * (1.0 + h * (1.0 - s)))
        late[MID, 1:9, :, lanes] = middle.astype(BF16).reshape(8, 16, 128)
        late[GHID, 1:9, :, lanes] = ghid.astype(BF16).reshape(8, 16, 128)
    halo = halo_copies(
        ((late.at[:, E], late.at[:, 0]), (late.at[:, 1], late.at[:, E + 1])),
        halo_send, halo_recv, count, me,
    )
    halo_start(halo, count, me)
    hear(1, twos)
    tell(3, fours)
    chip[HALF:, :] = jnp.zeros((CH * plane - HALF, 128), BF16)
    for i in range(5):
        filter_taps(4 * (1 - core) + i, late, padded, sums)

    own = pl.multiple_of(core * HALF, 8)
    other = pl.multiple_of((1 - core) * HALF, 8)
    to_core = pltpu.make_async_remote_copy(
        src_ref=sums.at[pl.ds(other, HALF)],
        dst_ref=from_core,
        send_sem=core_send,
        recv_sem=core_recv,
        device_id={"dom": partner},
    )
    to_core.start()
    for i in range(4):
        filter_taps(5 * core + i, late, padded, sums)
    to_core.wait_recv()
    chip[:HALF, :] = (from_core[...] + sums[pl.ds(own, HALF), :]).astype(BF16)

    def plane_copy(i):
        begin = pl.multiple_of(spot_at(ahead(i)) * CH, CH)
        return pltpu.make_async_remote_copy(
            src_ref=chip.at[pl.ds(begin, CH)],
            dst_ref=from_plane.at[i],
            send_sem=plane_send.at[i],
            recv_sem=plane_recv.at[i],
            device_id={"dom": device_at(ahead(i))},
        )

    hear(2, columns)
    for i in order:

        @pl.when(spot_at(ahead(i)) < live)
        def _():
            plane_copy(i).start()

    def last(field, band, flipped, target, base):
        for pair in range(4):
            lanes = slice(128 * pair, 128 * pair + 128)
            value = convolve(late_padded, field, band, pair, flipped)
            if flipped:
                value = value * alive
            value = value.reshape(8, 16, 128) + given[base, :, :, lanes].astype(F32)
            for b in range(2):
                target[b, :, :, lanes] = value[:, 8 * b : 8 * b + 8].astype(BF16)

    build_band(wb, band_b)
    build_flipped(wa, band_at)
    halo_wait(halo, count, me)
    for field in (MID, GHID):
        pad_inner(late[field, 1:9], sel, late_padded, field)
        pad_edge(late[field, 0], late[field, 9], sel_edge, late_padded, field)
    last(MID, band_b, False, out, FEAT)

    to_group = [
        pltpu.make_async_remote_copy(
            src_ref=groups.at[zhigh],
            dst_ref=groups.at[zhigh],
            send_sem=group_send.at[step - 1],
            recv_sem=group_recv.at[step - 1],
            device_id={"dom": at_group(step)},
        )
        for step in sorted(range(1, nhigh), key=lambda step: -min(step, nhigh - step))
    ]
    back = [
        pltpu.make_async_remote_copy(
            src_ref=full.at[core, spot],
            dst_ref=full.at[core, spot],
            send_sem=back_send.at[i],
            recv_sem=back_recv.at[i],
            device_id={"dom": device_at(behind(i))},
        )
        for i in range(len(steps))
    ]

    def forward(place):
        return pltpu.make_async_remote_copy(
            src_ref=full.at[core, place],
            dst_ref=full.at[core, place],
            send_sem=last_send.at[place],
            recv_sem=last_recv.at[place],
            device_id={"dom": partner},
        )

    hear(3, fours)

    @pl.when(spot < live)
    def _():
        total = chip[pl.ds(pl.multiple_of(spot * CH, CH), CH), :].astype(F32)
        for i in order:
            plane_copy(i).wait_recv()
        for i in range(len(steps)):
            total = total + from_plane[i].astype(F32)
        groups[zhigh] = total.astype(BF16)
        for copy in to_group:
            copy.start()

    last(GHID, band_at, True, gfeat, GOUT)

    @pl.when(spot < live)
    def _():
        for copy in to_group:
            copy.wait_recv()
        total = groups[0].astype(F32)
        for i in range(1, nhigh):
            total = total + groups[i].astype(F32)
        full[core, spot] = (total * scale).astype(BF16)
        for i in order:
            back[i].start()
        forward(spot).start()

    to_core.wait_send()
    for i in order:

        @pl.when(spot_at(ahead(i)) < live)
        def _():
            plane_copy(i).wait_send()

    for i in order[::-1]:

        @pl.when(spot_at(ahead(i)) < live)
        def _():
            back[i].wait_recv()
            forward(spot_at(ahead(i))).start()

    @pl.when(spot < live)
    def _():
        for copy in to_group:
            copy.wait_send()
        for copy in back:
            copy.wait_send()

    for place in range(live):
        forward(place).wait()


def finish(out_in, gfeat_in, full, out, gfeat, fa, fb, fa_here, fb_here, sems):
    copies = [
        pltpu.make_async_copy(out_in, out, sems.at[0]),
        pltpu.make_async_copy(gfeat_in, gfeat, sems.at[1]),
    ]
    for copy in copies:
        copy.start()
    for h in range(NCORE):
        rows = slice(h * HALF, h * HALF + HALF)
        value = full[h].reshape(full.shape[1] * CH, 128)[:HALF].astype(F32)
        fa_here[rows, :] = value[:, :C]
        fb_here[rows, :] = pltpu.roll(value, C, 1)[:, :C]
        for i, (here, there) in enumerate(((fa_here, fa), (fb_here, fb))):
            copy = pltpu.make_async_copy(here.at[rows], there.at[rows], sems.at[2 + 2 * h + i])
            copy.start()
            copies.append(copy)
    for copy in copies:
        copy.wait()


def on_device(ny, nz, features, weight_first, weight_second, neighbours, active, cotangent):
    count = ny * nz * NCORE
    scale = 1.0 / math.sqrt(2 * count * E**3)
    plane = ny * ZLOW
    nhigh = nz // ZLOW
    vmem = pl.BlockSpec(memory_space=pltpu.VMEM)
    hbm = pl.BlockSpec(memory_space=pltpu.HBM)
    dma = pltpu.SemaphoreType.DMA
    brick = jax.ShapeDtypeStruct(features.shape, BF16)
    whole = pltpu.VMEM(features.shape, BF16)
    taps = pltpu.VMEM(weight_first.shape, BF16)
    out, gfeat, full = pl.pallas_call(
        functools.partial(kernel, ny, nz, scale),
        out_shape=(brick, brick, jax.ShapeDtypeStruct((NCORE, plane, CH, 128), BF16)),
        in_specs=[hbm] * 6,
        out_specs=(vmem, vmem, vmem),
        scratch_shapes=[
            whole, whole, taps, taps,
            pltpu.SMEM(neighbours.shape, jnp.int32),
            pltpu.SMEM(active.shape, jnp.int32),
            pltpu.VMEM((2, 2, 2, E, 512), BF16),
            pltpu.VMEM((2, 8, 16, 512), BF16),
            pltpu.VMEM((3, 384, 128), BF16),
            pltpu.VMEM((3, 96, 32), BF16),
            pltpu.VMEM((2, 480, 640), BF16),
            pltpu.VMEM((9, 256, 128), BF16),
            pltpu.VMEM((9, 128, 256), BF16),
            pltpu.VMEM((9, 256, 128), BF16),
            pltpu.VMEM((9, 128, 256), BF16),
            pltpu.VMEM((2, 10, 16, 512), BF16),
            pltpu.VMEM((2, 480, 640), BF16),
            pltpu.VMEM((ROWS, 128), F32),
            pltpu.VMEM((HALF, 128), F32),
            pltpu.VMEM((plane * CH, 128), BF16),
            pltpu.VMEM((plane - 1, CH, 128), BF16),
            pltpu.VMEM((nhigh, CH, 128), BF16),
            dma((6,)), dma((4,)), dma((4,)),
            dma((2,)), dma((2,)),
            dma, dma,
            dma((plane - 1,)), dma((plane - 1,)),
            dma((nhigh - 1,)), dma((nhigh - 1,)),
            dma((plane - 1,)), dma((plane - 1,)),
            dma((plane,)), dma((plane,)),
            pltpu.SemaphoreType.REGULAR((4,)),
        ],
        compiler_params=pltpu.CompilerParams(
            collective_id=0, has_side_effects=True, vmem_limit_bytes=40 * 2**20
        ),
    )(
        *[
            pltpu.with_memory_space_constraint(value, pltpu.HBM)
            for value in (
                features, weight_first, weight_second, neighbours, active, cotangent
            )
        ]
    )
    grads = jax.ShapeDtypeStruct((ROWS, C), F32)
    out, gfeat, fa, fb = pl.pallas_call(
        finish,
        out_shape=(brick, brick, grads, grads),
        in_specs=[vmem] * 3,
        out_specs=(hbm,) * 4,
        scratch_shapes=[pltpu.VMEM((ROWS, C), F32), pltpu.VMEM((ROWS, C), F32), dma((6,))],
        compiler_params=pltpu.CompilerParams(vmem_limit_bytes=24 * 2**20),
    )(out, gfeat, full)
    return out, gfeat, fa.reshape(3, 3, 3, C, C), fb.reshape(3, 3, 3, C, C)


def solution(mesh):
    count = mesh.shape["dom"]
    return jax.shard_map(
        functools.partial(on_device, count // (NZ * NCORE), NZ),
        mesh=mesh,
        in_specs=(
            P(("scene", "dom"), None, None, None),
            P(),
            P(),
            P(("scene", "dom"), None),
            P(("scene", "dom")),
            P(("scene", "dom"), None, None, None),
        ),
        out_specs=(
            P(("scene", "dom"), None, None, None),
            P(("scene", "dom"), None, None, None),
            P("scene", None, None, None, None),
            P("scene", None, None, None, None),
        ),
        check_vma=False,
    )
```
